256 devices in a mesh: dom: 128 (over y, z, x), slab: 2 (over core).
Axes of the slice: x: 4, y: 4, z: 8, core: 2. Of those that a mesh axis runs over, the one named last changes fastest.
Arguments:
- node_coords: float32 [3, 360448], P(None, ('dom', 'slab')), may hold values from -6 to 6
- displacement: float32 [6, 360448], P(None, ('dom', 'slab')), may hold values from -6 to 6
- stress_operator: bfloat16 [24, 30, 262144], P(None, None, ('dom', 'slab')), may hold values from -1 to 1
- connectivity: int32 [10, 262144], P(None, ('dom', 'slab')), may hold values from 0 to 1791
- node_send: int32 [256, 3, 128], P(('dom', 'slab')), may hold values from 0 to 1407
- element_send: int32 [256, 3, 128], P(('dom', 'slab')), may hold values from 0 to 1023
- patch_elements: int32 [128, 49152], P(None, ('dom', 'slab')), may hold values from 0 to 1407
- patch_count: int32 [256, 192], P(('dom', 'slab')), may hold values from 1 to 128, 8192 in all within a row
Outputs:
- recovered: float32 [12, 49152], P(None, ('dom', 'slab'))
The draws below stay inside these ranges and needn't reach their ends.
Inputs may be any that keep to these rules, and one draw needn't show every extreme that they name: `patch_elements`: entries at slots beyond a patch's count are arbitrary. `patch_count`: on each partition the 192 counts sum to exactly 8192, and one of them is 128.
All inputs are finite; a program needn't handle non-finite values.
Results may differ from the reference program's by a relative error of at most 0.0003.
Values sent between devices are 32-bit elements; how exact they have to be, the bound alone decides.
No kernel may reach another device: no remote copies, remote signals or barrier semaphores. Data moves between devices by JAX's collectives and lax.ppermute only.
A program may use at most 64 MiB of HBM per device.

```python
import math
import jax
import jax.numpy as jnp
import numpy as np
from jax import lax

E_DEV = 1024
SLOTS = 128
NODE_DEV = 1408
P_DEV = 192
H_N = 128
H_E = 128
PAIRS_DEV = 8192
NODE_EXT = 1792
E_EXT = 1408
E_TOTAL = 262144
NODE_TOTAL = 360448
P_TOTAL = 49152
N_DOM = 128
N_SLAB = 2
DEVICES = 256


def place_ends(values, own_key, smallest, largest):
    longest = values.shape.index(max(values.shape))
    spots = []
    for shift in (0, 1):
        where = [jax.random.randint(jax.random.fold_in(own_key, axis), (), 0, length) for axis, length in enumerate(values.shape)]
        where[longest] = (where[longest] + shift) % values.shape[longest]
        spots.append(tuple(where))
    return values.at[spots[0]].set(smallest).at[spots[1]].set(largest)


def block_levels(stream_key, dims, shards, least, high):
    level, own = 1.0, jax.random.fold_in(stream_key, 6)
    for position, blocks in shards:
        heights = jnp.exp(jax.random.uniform(jax.random.fold_in(own, position), (blocks,), jnp.float32, least / len(shards), high / len(shards)))
        level = level * jnp.repeat(heights, dims[position] // blocks).reshape([-1 if axis == position else 1 for axis in range(len(dims))])
    return level


def profile(number_of, total, reach, slope):
    loads = [(1 << 20) // math.isqrt(rank ** slope) + 1 for rank in range(2, number_of + 1)]
    spare, given = total - reach - (number_of - 1), [1] * (number_of - 1)
    while spare > 0:
        free = [i for i in range(number_of - 1) if given[i] < reach]
        mass, left = sum([loads[i] for i in free]), spare
        for i in free:
            extra = min(reach - given[i], max(1, left * loads[i] // mass), spare)
            given[i] = given[i] + extra
            spare = spare - extra
    return np.array([reach] + given)


def ragged_sizes(key, amount, total, reach, lean):
    if amount == 2:
        one = jax.random.randint(key, (), max(1, total - reach), min(reach, total - 1) + 1)
        return jnp.stack([one, total - one])
    sizes = jnp.asarray(profile(amount, total, reach, lean), jnp.int32)
    twos = (amount - 1) // 2
    source_of, taker = sizes[1:1 + 2 * twos:2], sizes[2:2 + 2 * twos:2]
    slack = jnp.minimum(source_of - 1, reach - taker)
    moved = jax.random.randint(jax.random.fold_in(key, 1), (twos,), 0, 1 << 20) % (slack + 1)
    sizes = sizes.at[1:1 + 2 * twos:2].set(source_of - moved).at[2:2 + 2 * twos:2].set(taker + moved)
    return sizes[jax.random.permutation(jax.random.fold_in(key, 2), amount)]


def bell_draw(stream_key, shape, scale, reach, cuts=(), held_as=jnp.bfloat16):
    values = jax.random.normal(stream_key, shape, jnp.float32) * scale
    if len(cuts) > 0:
        values = block_levels(stream_key, shape, cuts, -0.22, 0.18) * values
    return jnp.clip(values, min=-reach, max=reach).astype(held_as)


def setup_inputs(seed: int = 0) -> dict:
    key_list = jax.random.split(jax.random.key(seed), 9)
    node_coords = bell_draw(key_list[0], (3, NODE_TOTAL), 1.0, 6.0, ((1, 256),), jnp.float32)
    displacement = bell_draw(key_list[1], (6, NODE_TOTAL), 1.0, 6.0, ((1, 256),), jnp.float32)
    stress_operator = bell_draw(key_list[2], (24, 30, E_TOTAL), 30 ** -0.5, 1.0, ((2, 256),))
    connectivity = place_ends(jax.random.randint(key_list[3], (10, E_TOTAL), 0, NODE_EXT), jax.random.fold_in(key_list[3], 1), 0, NODE_EXT - 1).astype(jnp.int32)
    node_send = place_ends(jax.random.randint(key_list[4], (DEVICES, 3, H_N), 0, NODE_DEV), jax.random.fold_in(key_list[4], 1), 0, NODE_DEV - 1).astype(jnp.int32)
    element_send = place_ends(jax.random.randint(key_list[5], (DEVICES, 3, H_E), 0, E_DEV), jax.random.fold_in(key_list[5], 1), 0, E_DEV - 1).astype(jnp.int32)
    patch_elements = place_ends(jax.random.randint(key_list[6], (SLOTS, P_TOTAL), 0, E_EXT), jax.random.fold_in(key_list[6], 1), 0, E_EXT - 1).astype(jnp.int32)
    patch_count = jax.vmap(lambda own: ragged_sizes(own, P_DEV, PAIRS_DEV, SLOTS, 2))(jax.random.split(key_list[7], DEVICES)).reshape((DEVICES, P_DEV)).astype(jnp.int32)
    return {"node_coords": node_coords, "displacement": displacement, "stress_operator": stress_operator, "connectivity": connectivity, "node_send": node_send, "element_send": element_send, "patch_elements": patch_elements, "patch_count": patch_count}


ridge_weight = 1.0

def shape_table():
    near = 0.5854101966249685
    far = 0.1381966011250105
    edge_pairs = ((0, 1), (1, 2), (0, 2), (0, 3), (1, 3), (2, 3))
    table_rows = []
    for corner in range(4):
        barycentric = [far, far, far, far]
        barycentric[corner] = near
        values = [barycentric[vertex_id] * (2.0 * barycentric[vertex_id] - 1.0) for vertex_id in range(4)]
        values = values + [4.0 * barycentric[first] * barycentric[second] for first, second in edge_pairs]
        table_rows.append(values)
    return jnp.array(table_rows, jnp.float32)

def element_blocks(extended, connectivity, operator):
    elem_count = connectivity.shape[1]
    gathered = extended[:, connectivity]
    qp_coords = jnp.einsum('qn,dne->qde', shape_table(), gathered[0:3], precision=lax.Precision.HIGHEST)
    elem_disp = gathered[3:9].reshape(2, 3, 10, elem_count).transpose(2, 1, 0, 3).reshape(30, 2, elem_count)
    stress = jnp.einsum('ske,kte->ste', operator.astype(jnp.float32), elem_disp, precision=lax.Precision.HIGHEST)
    stress = stress.reshape(4, 6, 2, elem_count).transpose(0, 2, 1, 3).reshape(48, elem_count)
    return jnp.concatenate([stress, qp_coords.reshape(12, elem_count)], axis=0)

def basis_terms(data, vertex):
    rest = data.shape[1:]
    stress = data[0:48].reshape((4, 12) + rest)
    coords = data[48:60].reshape((4, 3) + rest)
    offset = coords - vertex[None]
    ones_row = jnp.ones((4, 1) + rest, jnp.float32)
    return (jnp.concatenate([ones_row, offset], axis=1), stress)

def solve_first(gram, rhs):
    lower = [[None] * 4 for _ in range(4)]
    for row_id in range(4):
        for col_id in range(row_id + 1):
            total = gram[row_id, col_id]
            for inner in range(col_id):
                total = total - lower[row_id][inner] * lower[col_id][inner]
            if row_id == col_id:
                lower[row_id][col_id] = jnp.sqrt(total)
            else:
                lower[row_id][col_id] = total / lower[col_id][col_id]
    forward = []
    for row_id in range(4):
        total = rhs[row_id]
        for inner in range(row_id):
            total = total - lower[row_id][inner][None] * forward[inner]
        forward.append(total / lower[row_id][row_id][None])
    backward = [None] * 4
    for row_id in range(3, -1, -1):
        total = forward[row_id]
        for inner in range(row_id + 1, 4):
            total = total - lower[inner][row_id][None] * backward[inner]
        backward[row_id] = total / lower[row_id][row_id][None]
    return backward[0]

def fit_padded(blocks, patch_list, counts, vertex):
    data = blocks[:, patch_list]
    slot_ids = jnp.arange(patch_list.shape[0], dtype=jnp.int32)
    live = (slot_ids[:, None] < counts[None, :]).astype(jnp.float32)
    basis, stress = basis_terms(data, vertex[:, None, :])
    gram = jnp.einsum('qasp,qbsp,sp->abp', basis, basis, live, precision=lax.Precision.HIGHEST)
    rhs = jnp.einsum('qasp,qcsp,sp->acp', basis, stress, live, precision=lax.Precision.HIGHEST)
    gram = gram + ridge_weight * jnp.eye(4, dtype=jnp.float32)[:, :, None]
    return solve_first(gram, rhs)

def with_neighbours(own, blocks):
    devices = N_DOM * N_SLAB
    grid = blocks.reshape((N_DOM, N_SLAB) + blocks.shape[1:])
    from_prev = jnp.roll(grid[:, :, 1], 1, axis=0)
    from_next = jnp.roll(grid[:, :, 0], -1, axis=0)
    from_partner = grid[:, ::-1, 2]
    received = jnp.concatenate([from_prev, from_next, from_partner], axis=-1)
    received = received.reshape((devices,) + received.shape[2:])
    return jnp.concatenate([own, received], axis=-1)

def pick_rows(rows, lists):
    return jnp.stack([rows[:, lists[0]], rows[:, lists[1]], rows[:, lists[2]]])

def reference(node_coords, displacement, stress_operator, connectivity, node_send, element_send, patch_elements, patch_count):
    devices = N_DOM * N_SLAB
    node_rows = jnp.concatenate([node_coords, displacement], axis=0)
    node_rows = node_rows.reshape(9, devices, NODE_DEV).transpose(1, 0, 2)
    node_blocks = jax.vmap(pick_rows)(node_rows, node_send)
    extended_nodes = with_neighbours(node_rows, node_blocks)

    def one_partition(device_id):
        start = (device_id * E_DEV).astype(jnp.int32)
        operator = lax.dynamic_slice_in_dim(stress_operator, start, E_DEV, 2)
        links = lax.dynamic_slice_in_dim(connectivity, start, E_DEV, 1)
        return element_blocks(extended_nodes[device_id], links, operator)
    blocks = lax.map(one_partition, jnp.arange(devices, dtype=jnp.int32))
    sent = jax.vmap(pick_rows)(blocks, element_send)
    extended_blocks = with_neighbours(blocks, sent)

    def one_fit(device_id):
        start = (device_id * P_DEV).astype(jnp.int32)
        patch_list = lax.dynamic_slice_in_dim(patch_elements, start, P_DEV, 1)
        vertex = extended_nodes[device_id][0:3, 0:P_DEV]
        return fit_padded(extended_blocks[device_id], patch_list, patch_count[device_id], vertex)
    recovered = lax.map(one_fit, jnp.arange(devices, dtype=jnp.int32))
    return recovered.transpose(1, 0, 2).reshape(12, devices * P_DEV)
```

```python
import jax
import jax.numpy as jnp
import numpy as np
from jax import lax
from jax.experimental import pallas as pl
from jax.experimental.pallas import tpu as pltpu
from jax.sharding import PartitionSpec as P

RIDGE = 1.0
LANES = 128
VMEM = pl.BlockSpec(memory_space=pltpu.VMEM)
LIMIT = 24 * 1024 * 1024


def shape_table():
    near = 0.5854101966249685
    far = 0.1381966011250105
    edge_pairs = ((0, 1), (1, 2), (0, 2), (0, 3), (1, 3), (2, 3))
    table_rows = []
    for corner in range(4):
        barycentric = [far, far, far, far]
        barycentric[corner] = near
        values = [b * (2.0 * b - 1.0) for b in barycentric]
        values = values + [4.0 * barycentric[a] * barycentric[b] for a, b in edge_pairs]
        table_rows.append(values)
    return np.array(table_rows, np.float32)


SHAPE = shape_table()


def lane_gather(table, index):
    return jnp.take_along_axis(table, index, axis=1, mode="promise_in_bounds")


def rows8(ref, row, lanes):
    return jnp.broadcast_to(ref[pl.ds(row, 1), lanes], (8, LANES))


def node_pick_kernel(coords_ref, disp_ref, send_ref, prev_ref, next_ref, other_ref, table_ref):
    chunks = coords_ref.shape[1] // LANES
    for chunk in range(chunks):
        lanes = pl.ds(chunk * LANES, LANES)
        table_ref[chunk, 0:3, :] = coords_ref[:, lanes]
        table_ref[chunk, 3:9, :] = disp_ref[:, lanes]
    for side, out_ref in enumerate((prev_ref, next_ref, other_ref)):
        index = jnp.broadcast_to(send_ref[side], (8, LANES))
        low, high = index & 127, index >> 7
        first = jnp.zeros((8, LANES), jnp.float32)
        second = first
        for chunk in range(chunks):
            hit = high == chunk
            first = jnp.where(hit, lane_gather(table_ref[chunk, 0:8, :], low), first)
            second = jnp.where(hit, lane_gather(table_ref[chunk, 8:16, :], low), second)
        out_ref[0:8, :] = first
        out_ref[8:9, :] = second[0:1]


def node_pick(coords, disp, send):
    out = jax.ShapeDtypeStruct((9, LANES), jnp.float32)
    return pl.pallas_call(
        node_pick_kernel,
        out_shape=(out, out, out),
        in_specs=[VMEM] * 3,
        out_specs=(VMEM,) * 3,
        scratch_shapes=[pltpu.VMEM((coords.shape[1] // LANES, 16, LANES), jnp.float32)],
        compiler_params=pltpu.CompilerParams(vmem_limit_bytes=LIMIT),
        name="node_pick",
    )(coords, disp, send)


def own_gather_kernel(coords_ref, disp_ref, conn_ref, out_ref, table_ref):
    chunks = coords_ref.shape[1] // LANES
    for chunk in range(chunks):
        lanes = pl.ds(chunk * LANES, LANES)
        table_ref[chunk, 0:3, :] = coords_ref[:, lanes]
        table_ref[chunk, 3:9, :] = disp_ref[:, lanes]

    def group(block, carry):
        lanes = pl.ds(pl.multiple_of(block * LANES, LANES), LANES)
        for node in range(10):
            index = rows8(conn_ref, node, lanes)
            low, high = index & 127, index >> 7
            first = jnp.zeros((8, LANES), jnp.float32)
            second = first
            for chunk in range(chunks):
                hit = high == chunk
                first = jnp.where(hit, lane_gather(table_ref[chunk, 0:8, :], low), first)
                second = jnp.where(hit, lane_gather(table_ref[chunk, 8:16, :], low), second)
            out_ref[node, 0:8, lanes] = first
            out_ref[node, 8:16, lanes] = second
        return carry

    lax.fori_loop(0, conn_ref.shape[1] // LANES, group, 0)


def own_gather(coords, disp, conn):
    return pl.pallas_call(
        own_gather_kernel,
        out_shape=jax.ShapeDtypeStruct((10, 16, conn.shape[1]), jnp.float32),
        in_specs=[VMEM] * 3,
        out_specs=VMEM,
        scratch_shapes=[pltpu.VMEM((coords.shape[1] // LANES, 16, LANES), jnp.float32)],
        compiler_params=pltpu.CompilerParams(vmem_limit_bytes=LIMIT),
        cost_estimate=pl.CostEstimate(flops=20000000, bytes_accessed=4000000, transcendentals=0),
        name="own_gather",
    )(coords, disp, conn)


def block_kernel(
    first_halo, own_ref, conn_ref, oper_hbm, h0_ref, h1_ref, h2_ref, send_ref,
    blk_ref, prev_ref, next_ref, other_ref, table_ref, full_ref, oper_ref, sem,
):
    copy = pltpu.make_async_copy(oper_hbm, oper_ref, sem)
    copy.start()
    for side, ref in enumerate((h0_ref, h1_ref, h2_ref)):
        table_ref[side, 0:9, :] = ref[...]
    sub = lax.broadcasted_iota(jnp.int32, (8, LANES), 0)
    groups = conn_ref.shape[1] // LANES

    def fill(block, carry):
        lanes = pl.ds(pl.multiple_of(block * LANES, LANES), LANES)
        for node in range(10):
            index = rows8(conn_ref, node, lanes)
            low, high = index & 127, index >> 7
            first = own_ref[node, 0:8, lanes]
            second = own_ref[node, 8:16, lanes]
            for side in range(3):
                hit = high == first_halo + side
                first = jnp.where(hit, lane_gather(table_ref[side, 0:8, :], low), first)
                second = jnp.where(hit, lane_gather(table_ref[side, 8:16, :], low), second)
            full_ref[node, 0:8, lanes] = first
            full_ref[node, 8:16, lanes] = second
        return carry

    lax.fori_loop(0, groups, fill, 0)
    copy.wait()

    def stress(block, carry):
        lanes = pl.ds(pl.multiple_of(block * LANES, LANES), LANES)
        totals = [jnp.zeros((24, LANES), jnp.float32) for _ in range(2)]
        for node in range(10):
            for comp in range(3):
                oper = oper_ref[3 * node + comp, :, lanes].astype(jnp.float32)
                for step in range(2):
                    value = full_ref[node, pl.ds(3 + 3 * step + comp, 1), lanes]
                    totals[step] = totals[step] + oper * value
        blk_ref[0:24, lanes] = totals[0]
        blk_ref[24:48, lanes] = totals[1]
        nodes = [full_ref[node, 0:8, lanes] for node in range(10)]
        points = []
        for quad in range(4):
            total = nodes[0] * SHAPE[quad, 0]
            for node in range(1, 10):
                total = total + nodes[node] * SHAPE[quad, node]
            points.append(total)
        blk_ref[48:56, lanes] = jnp.where(sub < 4, points[0], pltpu.roll(points[1], 4, 0))
        blk_ref[56:64, lanes] = jnp.where(sub < 4, points[2], pltpu.roll(points[3], 4, 0))
        return carry

    lax.fori_loop(0, groups, stress, 0)
    for side, out_ref in enumerate((prev_ref, next_ref, other_ref)):
        index = jnp.broadcast_to(send_ref[side], (8, LANES))
        low, high = index & 127, index >> 7
        hits = [high == chunk for chunk in range(groups)]
        for row in range(0, 64, 8):
            total = jnp.zeros((8, LANES), jnp.float32)
            for chunk in range(groups):
                piece = blk_ref[row:row + 8, chunk * LANES:(chunk + 1) * LANES]
                total = jnp.where(hits[chunk], lane_gather(piece, low), total)
            out_ref[row:row + 8, :] = total


def make_blocks(own, conn, oper, halos, send, first_halo):
    elems = conn.shape[1]
    out = jax.ShapeDtypeStruct((64, LANES), jnp.float32)

    def kernel(*refs):
        block_kernel(first_halo, *refs)

    return pl.pallas_call(
        kernel,
        out_shape=(jax.ShapeDtypeStruct((64, elems), jnp.float32), out, out, out),
        in_specs=[VMEM, VMEM, pl.BlockSpec(memory_space=pl.ANY)] + [VMEM] * 4,
        out_specs=(VMEM,) * 4,
        scratch_shapes=[
            pltpu.VMEM((3, 16, LANES), jnp.float32),
            pltpu.VMEM((10, 16, elems), jnp.float32),
            pltpu.VMEM(oper.shape, oper.dtype),
            pltpu.SemaphoreType.DMA,
        ],
        compiler_params=pltpu.CompilerParams(vmem_limit_bytes=LIMIT),
        name="make_blocks",
    )(own, conn, oper, *halos, send)


def add_points(sub, piece):
    pair = jnp.where(sub >= 6, piece[0], piece[1])
    later = jnp.where(sub >= 4, piece[1], piece[2])
    return piece[0] + pltpu.roll(pair, 2, 0) + pltpu.roll(later, 4, 0) + pltpu.roll(piece[2], 6, 0)


def moment_rows(sub, ref, lanes, out_ref, out_lanes):
    spread = []
    for dim in range(3):
        rows = [rows8(ref, 48 + 4 * quad + dim, lanes) for quad in range(4)]
        spread.append([jnp.where(sub < 6 - 2 * k, rows[k], rows[k + 1]) for k in range(3)])
    for step in range(2):
        piece = [ref[24 * step + 8 * k:24 * step + 8 * k + 8, lanes] for k in range(3)]
        base = 32 * step
        out_ref[base:base + 8, out_lanes] = add_points(sub, piece)
        for dim in range(3):
            scaled = [piece[k] * spread[dim][k] for k in range(3)]
            out_ref[base + 8 * dim + 8:base + 8 * dim + 16, out_lanes] = add_points(sub, scaled)
    pair = [ref[48:56, lanes], ref[56:64, lanes]]
    out_ref[64:72, out_lanes] = pair[0] + pair[1]
    out_ref[72:80, out_lanes] = pair[0] * pair[0] + pair[1] * pair[1]
    for shift in (1, 2):
        total = pair[0] * pltpu.roll(pair[0], 8 - shift, 0) + pair[1] * pltpu.roll(pair[1], 8 - shift, 0)
        out_ref[72 + 8 * shift:80 + 8 * shift, out_lanes] = total


def summed_over(moments, weights):
    total = None
    rest = moments
    for part in range(3):
        piece = rest.astype(jnp.bfloat16)
        if part < 2:
            rest = rest - piece.astype(jnp.float32)
        term = lax.dot_general(
            piece, weights, (((1,), (1,)), ((), ())), preferred_element_type=jnp.float32
        )
        total = term if total is None else total + term
    return total


def weight_kernel(list_ref, count_ref, weight_ref, index_ref, hist_ref):
    patches, slots = list_ref.shape
    counts = count_ref[...].astype(jnp.float32)
    diagonal = lax.broadcasted_iota(jnp.int32, (patches, patches), 0) == lax.broadcasted_iota(
        jnp.int32, (patches, patches), 1
    )
    spread = jnp.where(diagonal, jnp.broadcast_to(counts, (patches, patches)), 0.0)
    limits = jnp.dot(
        spread.astype(jnp.bfloat16),
        jnp.ones((patches, slots), jnp.bfloat16),
        preferred_element_type=jnp.float32,
    ).astype(jnp.int32)
    slot = lax.broadcasted_iota(jnp.int32, (patches, slots), 1)
    index_ref[...] = jnp.where(slot < limits, list_ref[...], 4095)
    low_ids = lax.broadcasted_iota(jnp.int32, (LANES, slots), 0)
    high_ids = lax.broadcasted_iota(jnp.int32, (16, slots), 0)
    width = 8

    def group(block, carry):
        start = pl.multiple_of(block * width, width)
        listed = index_ref[pl.ds(start, width), :]
        low, high = listed & 127, listed >> 7
        for patch in range(width):
            low_hit = low_ids == jnp.broadcast_to(low[patch:patch + 1], (LANES, slots))
            high_hit = high_ids == jnp.broadcast_to(high[patch:patch + 1], (16, slots))
            hist = lax.dot_general(
                jnp.where(high_hit, 1.0, 0.0).astype(jnp.bfloat16),
                jnp.where(low_hit, 1.0, 0.0).astype(jnp.bfloat16),
                (((1,), (1,)), ((), ())),
                preferred_element_type=jnp.float32,
            )
            hist_ref[pl.ds(pl.multiple_of(start * 16, LANES) + 16 * patch, 16), :] = hist
        return carry

    lax.fori_loop(0, patches // width, group, 0)
    for chunk in range(weight_ref.shape[1] // LANES):
        column = hist_ref[pl.ds(chunk, patches, stride=16), :]
        weight_ref[:, chunk * LANES:(chunk + 1) * LANES] = column.astype(jnp.bfloat16)


def make_weights(listed, counts, width):
    patches, slots = listed.shape
    return pl.pallas_call(
        weight_kernel,
        out_shape=jax.ShapeDtypeStruct((patches, width), jnp.bfloat16),
        in_specs=[VMEM] * 2,
        out_specs=VMEM,
        scratch_shapes=[
            pltpu.VMEM((patches, slots), jnp.int32),
            pltpu.VMEM((patches * 16, LANES), jnp.float32),
        ],
        compiler_params=pltpu.CompilerParams(vmem_limit_bytes=LIMIT),
        cost_estimate=pl.CostEstimate(flops=20000000, bytes_accessed=8000000, transcendentals=0),
        name="make_weights",
    )(listed, counts)


def own_sum_kernel(blk_ref, weight_ref, sum_ref, moment_ref):
    sub = lax.broadcasted_iota(jnp.int32, (8, LANES), 0)
    elems = blk_ref.shape[1]

    def group(block, carry):
        lanes = pl.ds(pl.multiple_of(block * LANES, LANES), LANES)
        moment_rows(sub, blk_ref, lanes, moment_ref, lanes)
        return carry

    lax.fori_loop(0, elems // LANES, group, 0)
    sum_ref[...] = summed_over(moment_ref[...], weight_ref[:, 0:elems])


def own_sums(blk, weights):
    return pl.pallas_call(
        own_sum_kernel,
        out_shape=jax.ShapeDtypeStruct((96, weights.shape[0]), jnp.float32),
        in_specs=[VMEM] * 2,
        out_specs=VMEM,
        scratch_shapes=[pltpu.VMEM((96, blk.shape[1]), jnp.float32)],
        compiler_params=pltpu.CompilerParams(vmem_limit_bytes=LIMIT),
        cost_estimate=pl.CostEstimate(flops=20000000, bytes_accessed=4000000, transcendentals=0),
        name="own_sums",
    )(blk, weights)


def fit_kernel(sum_ref, weight_ref, h0_ref, h1_ref, h2_ref, vertex_ref, count_ref, out_ref, moment_ref, total_ref):
    sub = lax.broadcasted_iota(jnp.int32, (8, LANES), 0)
    for side, ref in enumerate((h0_ref, h1_ref, h2_ref)):
        moment_rows(sub, ref, slice(0, LANES), moment_ref, slice(side * LANES, (side + 1) * LANES))
    width = moment_ref.shape[1]
    own = weight_ref.shape[1] - width
    patches = weight_ref.shape[0]
    total_ref[...] = sum_ref[...] + summed_over(moment_ref[...], weight_ref[:, own:own + width])

    def row(ref, start):
        return jnp.broadcast_to(ref[start:start + 1, 0:patches], (8, patches))

    def both(start):
        return row(total_ref, start) + row(total_ref, start + 4)

    points = 4.0 * row(count_ref, 0).astype(jnp.float32)
    vertex = [row(vertex_ref, dim) for dim in range(3)]
    sum_x = [both(64 + dim) for dim in range(3)]
    sum_xx = {
        (0, 0): both(72), (1, 1): both(73), (2, 2): both(74),
        (0, 1): both(80), (1, 2): both(81), (0, 2): both(88),
    }
    gram = {(0, 0): points + RIDGE}
    for a in range(3):
        gram[0, a + 1] = sum_x[a] - points * vertex[a]
        for b in range(a, 3):
            value = sum_xx[a, b] - vertex[a] * sum_x[b] - sum_x[a] * vertex[b] + points * vertex[a] * vertex[b]
            gram[a + 1, b + 1] = value + RIDGE if a == b else value
    rhs = []
    for step in range(2):
        base = total_ref[32 * step:32 * step + 8, :]
        rest = [total_ref[32 * step + 8 * dim + 8:32 * step + 8 * dim + 16, :] for dim in range(3)]
        rhs.append([base] + [rest[dim] - vertex[dim] * base for dim in range(3)])
    for pivot in (3, 2, 1):
        inverse = 1.0 / gram[pivot, pivot]
        for other in range(pivot):
            factor = gram[other, pivot] * inverse
            for column in range(other, pivot):
                gram[other, column] = gram[other, column] - factor * gram[column, pivot]
            for step in range(2):
                rhs[step][other] = rhs[step][other] - factor * rhs[step][pivot]
    inverse = 1.0 / gram[0, 0]
    for step in range(2):
        out_ref[6 * step:6 * step + 6, :] = (rhs[step][0] * inverse)[0:6]


def fit(sums, weights, halos, coords, counts):
    patches = weights.shape[0]
    return pl.pallas_call(
        fit_kernel,
        out_shape=jax.ShapeDtypeStruct((12, patches), jnp.float32),
        in_specs=[VMEM] * 7,
        out_specs=VMEM,
        scratch_shapes=[
            pltpu.VMEM((96, 3 * LANES), jnp.float32),
            pltpu.VMEM((96, patches), jnp.float32),
        ],
        compiler_params=pltpu.CompilerParams(vmem_limit_bytes=LIMIT),
        name="fit",
    )(sums, weights, *halos, coords, counts)


def exchange(to_prev, to_next, to_other):
    count = lax.axis_size("dom")
    up = [(i, (i + 1) % count) for i in range(count)]
    down = [(j, i) for i, j in up]
    swap = [(0, 1), (1, 0)]
    from_prev = lax.ppermute(to_next, "dom", up)
    from_next = lax.ppermute(to_prev, "dom", down)
    from_other = lax.ppermute(to_other, "slab", swap)
    return from_prev, from_next, from_other


def local(coords, disp, oper, conn, node_send, element_send, patch_elements, patch_count):
    node_send = node_send.transpose(1, 0, 2)
    element_send = element_send.transpose(1, 0, 2)
    oper = oper.transpose(1, 0, 2)
    listed = patch_elements.T
    picked = node_pick(coords, disp, node_send)
    halos = exchange(*picked)
    own = own_gather(coords, disp, conn)
    blk, *picked = make_blocks(own, conn, oper, halos, element_send, coords.shape[1] // LANES)
    weights = make_weights(listed, patch_count, conn.shape[1] + 3 * LANES)
    halos = exchange(*picked)
    sums = own_sums(blk, weights)
    return fit(sums, weights, halos, coords, patch_count)


def solution(mesh):
    both = ("dom", "slab")
    in_specs = (
        P(None, both),
        P(None, both),
        P(None, None, both),
        P(None, both),
        P(both, None, None),
        P(both, None, None),
        P(None, both),
        P(both, None),
    )
    return jax.shard_map(local, mesh=mesh, in_specs=in_specs, out_specs=P(None, both), check_vma=False)
```

```python
import jax
import jax.numpy as jnp
import numpy as np
from jax import lax
from jax.experimental import pallas as pl
from jax.experimental.pallas import tpu as pltpu
from jax.sharding import PartitionSpec as P

RIDGE = 1.0
LANES = 128
VMEM = pl.BlockSpec(memory_space=pltpu.VMEM)
HBM = pl.BlockSpec(memory_space=pltpu.HBM)
UNROLL = 2
WIDTH = 64
LIMIT = 24 * 1024 * 1024


def shape_table():
    near = 0.5854101966249685
    far = 0.1381966011250105
    edge_pairs = ((0, 1), (1, 2), (0, 2), (0, 3), (1, 3), (2, 3))
    table_rows = []
    for corner in range(4):
        barycentric = [far, far, far, far]
        barycentric[corner] = near
        values = [b * (2.0 * b - 1.0) for b in barycentric]
        values = values + [4.0 * barycentric[a] * barycentric[b] for a, b in edge_pairs]
        table_rows.append(values)
    return np.array(table_rows, np.float32)


SHAPE = shape_table()


def lane_gather(table, index):
    return jnp.take_along_axis(table, index, axis=1, mode="promise_in_bounds")


def rows8(ref, row, lanes):
    return jnp.broadcast_to(ref[pl.ds(row, 1), lanes], (8, LANES))


def start_all(pairs, sems):
    copies = [pltpu.make_async_copy(src, dst, sems.at[k]) for k, (src, dst) in enumerate(pairs)]
    for copy in copies:
        copy.start()
    return copies


def ninth_row(sub, table, low, high, chunks):
    total = jnp.zeros((8, LANES), jnp.float32)
    for start in range(0, chunks, 8):
        piece = lane_gather(table[start:start + 8, :], low)
        total = jnp.where(high == sub + start, piece, total)
    return total


def node_pick_kernel(
    coords_hbm, disp_hbm, send_hbm, conn_hbm,
    prev_ref, next_ref, other_ref, table_ref, ninth_ref, coords_ref, conn_ref,
    disp_ref, send_ref, sems,
):
    pairs = ((coords_hbm, coords_ref), (disp_hbm, disp_ref), (send_hbm, send_ref), (conn_hbm, conn_ref))
    copies = start_all(pairs, sems)
    for copy in copies[0:3]:
        copy.wait()
    sub = lax.broadcasted_iota(jnp.int32, (8, LANES), 0)
    chunks = table_ref.shape[0]
    ninth_ref[8:16, :] = jnp.zeros((8, LANES), jnp.float32)
    for chunk in range(chunks):
        lanes = pl.ds(chunk * LANES, LANES)
        table_ref[chunk, 0:3, :] = coords_ref[:, lanes]
        table_ref[chunk, 3:8, :] = disp_ref[0:5, lanes]
        ninth_ref[chunk:chunk + 1, :] = disp_ref[5:6, lanes]
    for side, out_ref in enumerate((prev_ref, next_ref, other_ref)):
        index = jnp.broadcast_to(send_ref[side], (8, LANES))
        low, high = index & 127, index >> 7
        first = jnp.zeros((8, LANES), jnp.float32)
        for chunk in range(chunks):
            first = jnp.where(high == chunk, lane_gather(table_ref[chunk], low), first)
        out_ref[0:8, :] = first
        last = ninth_row(sub, ninth_ref, low, high, chunks)
        out_ref[8:9, :] = jnp.sum(last, axis=0, keepdims=True)
    copies[3].wait()


def node_pick(coords, disp, send, conn):
    out = jax.ShapeDtypeStruct((9, LANES), jnp.float32)
    chunks = coords.shape[1] // LANES
    return pl.pallas_call(
        node_pick_kernel,
        out_shape=(
            out, out, out,
            jax.ShapeDtypeStruct((chunks, 8, LANES), jnp.float32),
            jax.ShapeDtypeStruct((16, LANES), jnp.float32),
            jax.ShapeDtypeStruct(coords.shape, coords.dtype),
            jax.ShapeDtypeStruct(conn.shape, conn.dtype),
        ),
        in_specs=[HBM] * 4,
        out_specs=(VMEM,) * 7,
        scratch_shapes=[
            pltpu.VMEM(disp.shape, disp.dtype),
            pltpu.VMEM(send.shape, send.dtype),
            pltpu.SemaphoreType.DMA((4,)),
        ],
        compiler_params=pltpu.CompilerParams(vmem_limit_bytes=LIMIT),
        name="node_pick",
    )(coords, disp, send, conn)


def own_gather_kernel(
    table_ref, ninth_ref, conn_ref, oper_hbm, list_hbm, count_hbm, send_hbm,
    first_ref, last_ref, oper_ref, list_ref, count_ref, send_ref, sems,
):
    pairs = ((oper_hbm, oper_ref), (list_hbm, list_ref), (count_hbm, count_ref), (send_hbm, send_ref))
    copies = start_all(pairs, sems)
    sub = lax.broadcasted_iota(jnp.int32, (8, LANES), 0)
    chunks = table_ref.shape[0]

    def group(block, carry):
        lanes = pl.ds(pl.multiple_of(block * LANES, LANES), LANES)
        for node in range(10):
            index = rows8(conn_ref, node, lanes)
            low, high = index & 127, index >> 7
            first = jnp.zeros((8, LANES), jnp.float32)
            for chunk in range(chunks):
                first = jnp.where(high == chunk, lane_gather(table_ref[chunk], low), first)
            first_ref[node, :, lanes] = first
            last = ninth_row(sub, ninth_ref, low, high, chunks)
            last_ref[node:node + 1, lanes] = jnp.sum(last, axis=0, keepdims=True)
        return carry

    lax.fori_loop(0, conn_ref.shape[1] // LANES, group, 0)
    for copy in copies:
        copy.wait()


def own_gather(table, ninth, conn, oper, listed, counts, send):
    elems = conn.shape[1]
    copied = [jax.ShapeDtypeStruct(x.shape, x.dtype) for x in (oper, listed, counts, send)]
    return pl.pallas_call(
        own_gather_kernel,
        out_shape=(
            jax.ShapeDtypeStruct((10, 8, elems), jnp.float32),
            jax.ShapeDtypeStruct((10, elems), jnp.float32),
            *copied,
        ),
        in_specs=[VMEM] * 3 + [HBM] * 4,
        out_specs=(VMEM,) * 6,
        scratch_shapes=[pltpu.SemaphoreType.DMA((4,))],
        compiler_params=pltpu.CompilerParams(vmem_limit_bytes=LIMIT),
        cost_estimate=pl.CostEstimate(flops=20000000, bytes_accessed=4000000, transcendentals=0),
        name="own_gather",
    )(table, ninth, conn, oper, listed, counts, send)


def block_kernel(
    first_halo, first_ref, last_ref, conn_ref, oper_ref, h0_ref, h1_ref, h2_ref, send_ref,
    blk_ref, prev_ref, next_ref, other_ref, ninth_ref, full_ref,
):
    halos = (h0_ref, h1_ref, h2_ref)
    for side, ref in enumerate(halos):
        ninth_ref[side:side + 1, :] = ref[8:9, :]
    sub = lax.broadcasted_iota(jnp.int32, (8, LANES), 0)
    groups = conn_ref.shape[1] // LANES

    def group(block, slot):
        lanes = pl.ds(pl.multiple_of(block * LANES, LANES), LANES)
        corners, edges = [], []
        for node in range(10):
            index = rows8(conn_ref, node, lanes)
            low, high = index & 127, index >> 7
            first = first_ref[node, :, lanes]
            for side in range(3):
                first = jnp.where(high == first_halo + side, lane_gather(halos[side][0:8, :], low), first)
            (corners if node < 4 else edges).append(first)
            full_ref[slot, node, 0:8, :] = first
            last = jnp.where(high == sub + first_halo, lane_gather(ninth_ref[...], low), 0.0)
            full_ref[slot, node, 8:16, :] = jnp.where(sub == 3, rows8(last_ref, node, lanes), last)
        totals = [[jnp.zeros((8, LANES), jnp.float32) for _ in range(3)] for _ in range(2)]
        for node in range(10):
            for comp in range(3):
                oper = oper_ref[3 * node + comp, :, lanes].astype(jnp.float32)
                for step in range(2):
                    row = 3 + 3 * step + comp
                    value = jnp.broadcast_to(full_ref[slot, node, row:row + 1, :], (8, LANES))
                    if row == 8:
                        for extra in (9, 10, 11):
                            value = value + jnp.broadcast_to(full_ref[slot, node, extra:extra + 1, :], (8, LANES))
                    for part in range(3):
                        totals[step][part] = totals[step][part] + oper[8 * part:8 * part + 8] * value
        for step in range(2):
            for part in range(3):
                row = 24 * step + 8 * part
                blk_ref[row:row + 8, lanes] = totals[step][part]
        points = []
        for quad in range(4):
            total = corners[0] * SHAPE[quad, 0]
            for node in range(1, 10):
                total = total + (corners + edges)[node] * SHAPE[quad, node]
            points.append(total)
        blk_ref[48:56, lanes] = jnp.where(sub < 4, points[0], pltpu.roll(points[1], 4, 0))
        blk_ref[56:64, lanes] = jnp.where(sub < 4, points[2], pltpu.roll(points[3], 4, 0))

    def pair(block, carry):
        for slot in range(UNROLL):
            group(block * UNROLL + slot, slot)
        return carry

    lax.fori_loop(0, groups // UNROLL, pair, 0)
    for side, out_ref in enumerate((prev_ref, next_ref, other_ref)):
        index = jnp.broadcast_to(send_ref[side], (8, LANES))
        low, high = index & 127, index >> 7
        hits = [high == chunk for chunk in range(groups)]
        for row in range(0, 64, 8):
            total = jnp.zeros((8, LANES), jnp.float32)
            for chunk in range(groups):
                piece = blk_ref[row:row + 8, chunk * LANES:(chunk + 1) * LANES]
                total = jnp.where(hits[chunk], lane_gather(piece, low), total)
            out_ref[row:row + 8, :] = total


def make_blocks(first, last, conn, oper, halos, send, first_halo):
    elems = conn.shape[1]
    out = jax.ShapeDtypeStruct((64, LANES), jnp.float32)

    def kernel(*refs):
        block_kernel(first_halo, *refs)

    return pl.pallas_call(
        kernel,
        out_shape=(jax.ShapeDtypeStruct((64, elems), jnp.float32), out, out, out),
        in_specs=[VMEM] * 8,
        out_specs=(VMEM,) * 4,
        scratch_shapes=[
            pltpu.VMEM((8, LANES), jnp.float32),
            pltpu.VMEM((UNROLL, 10, 16, LANES), jnp.float32),
        ],
        compiler_params=pltpu.CompilerParams(vmem_limit_bytes=LIMIT),
        name="make_blocks",
    )(first, last, conn, oper, *halos, send)


def add_points(sub, piece):
    pair = jnp.where(sub >= 6, piece[0], piece[1])
    later = jnp.where(sub >= 4, piece[1], piece[2])
    return piece[0] + pltpu.roll(pair, 2, 0) + pltpu.roll(later, 4, 0) + pltpu.roll(piece[2], 6, 0)


def moment_rows(sub, ref, lanes, out_ref, out_lanes):
    spread = []
    for dim in range(3):
        rows = [rows8(ref, 48 + 4 * quad + dim, lanes) for quad in range(4)]
        spread.append([jnp.where(sub < 6 - 2 * k, rows[k], rows[k + 1]) for k in range(3)])
    for step in range(2):
        piece = [ref[24 * step + 8 * k:24 * step + 8 * k + 8, lanes] for k in range(3)]
        base = 32 * step
        out_ref[base:base + 8, out_lanes] = add_points(sub, piece)
        for dim in range(3):
            scaled = [piece[k] * spread[dim][k] for k in range(3)]
            out_ref[base + 8 * dim + 8:base + 8 * dim + 16, out_lanes] = add_points(sub, scaled)
    pair = [ref[48:56, lanes], ref[56:64, lanes]]
    out_ref[64:72, out_lanes] = pair[0] + pair[1]
    out_ref[72:80, out_lanes] = pair[0] * pair[0] + pair[1] * pair[1]
    for shift in (1, 2):
        total = pair[0] * pltpu.roll(pair[0], 8 - shift, 0) + pair[1] * pltpu.roll(pair[1], 8 - shift, 0)
        out_ref[72 + 8 * shift:80 + 8 * shift, out_lanes] = total


def summed_over(moments, weights, weight_dim):
    total = None
    rest = moments
    for part in range(3):
        piece = rest.astype(jnp.bfloat16)
        if part < 2:
            rest = rest - piece.astype(jnp.float32)
        term = lax.dot_general(
            piece, weights, (((1,), (weight_dim,)), ((), ())), preferred_element_type=jnp.float32
        )
        total = term if total is None else total + term
    return total


def sum_kernel(
    list_ref, count_ref, blk_ref, sum_ref, halo_ref, index_ref, hist_ref, weight_ref, moment_ref
):
    patches, slots = list_ref.shape
    counts = count_ref[...].astype(jnp.float32)
    diagonal = lax.broadcasted_iota(jnp.int32, (patches, patches), 0) == lax.broadcasted_iota(
        jnp.int32, (patches, patches), 1
    )
    spread = jnp.where(diagonal, jnp.broadcast_to(counts, (patches, patches)), 0.0)
    limits = jnp.dot(
        spread.astype(jnp.bfloat16),
        jnp.ones((patches, slots), jnp.bfloat16),
        preferred_element_type=jnp.float32,
    ).astype(jnp.int32)
    slot = lax.broadcasted_iota(jnp.int32, (patches, slots), 1)
    index_ref[...] = jnp.where(slot < limits, list_ref[...], 4095)
    low_ids = lax.broadcasted_iota(jnp.int32, (LANES, slots), 0)
    high_ids = lax.broadcasted_iota(jnp.int32, (16, slots), 0)
    width = WIDTH

    def group(block, carry):
        start = pl.multiple_of(block * width, width)
        listed = index_ref[pl.ds(start, width), :]
        low, high = listed & 127, listed >> 7
        for patch in range(width):
            low_hit = low_ids == jnp.broadcast_to(low[patch:patch + 1], (LANES, slots))
            high_hit = high_ids == jnp.broadcast_to(high[patch:patch + 1], (16, slots))
            hist = lax.dot_general(
                jnp.where(high_hit, 1.0, 0.0).astype(jnp.float8_e4m3fn),
                jnp.where(low_hit, 1.0, 0.0).astype(jnp.float8_e4m3fn),
                (((1,), (1,)), ((), ())),
                preferred_element_type=jnp.float32,
            )
            hist_ref[pl.ds(pl.multiple_of(start * 16, LANES) + 16 * patch, 16), :] = hist
        return carry

    lax.fori_loop(0, patches // width, group, 0)
    elems = blk_ref.shape[1]
    chunks = elems // LANES
    for chunk in range(chunks + 3):
        column = hist_ref[pl.ds(chunk, patches, stride=16), :]
        if chunk < chunks:
            weight_ref[:, chunk * LANES:(chunk + 1) * LANES] = column.astype(jnp.bfloat16)
        else:
            row = (chunk - chunks) * LANES
            halo_ref[row:row + LANES, :] = column.T.astype(jnp.bfloat16)
    sub = lax.broadcasted_iota(jnp.int32, (8, LANES), 0)

    def moments(block, carry):
        lanes = pl.ds(pl.multiple_of(block * LANES, LANES), LANES)
        moment_rows(sub, blk_ref, lanes, moment_ref, lanes)
        return carry

    lax.fori_loop(0, chunks, moments, 0)
    sum_ref[...] = summed_over(moment_ref[...], weight_ref[...], 1)


def own_sums(listed, counts, blk):
    patches, slots = listed.shape
    elems = blk.shape[1]
    return pl.pallas_call(
        sum_kernel,
        out_shape=(
            jax.ShapeDtypeStruct((96, patches), jnp.float32),
            jax.ShapeDtypeStruct((3 * LANES, patches), jnp.bfloat16),
        ),
        in_specs=[VMEM] * 3,
        out_specs=(VMEM,) * 2,
        scratch_shapes=[
            pltpu.VMEM((patches, slots), jnp.int32),
            pltpu.VMEM((patches * 16, LANES), jnp.float32),
            pltpu.VMEM((patches, elems), jnp.bfloat16),
            pltpu.VMEM((96, elems), jnp.float32),
        ],
        compiler_params=pltpu.CompilerParams(vmem_limit_bytes=LIMIT),
        cost_estimate=pl.CostEstimate(flops=40000000, bytes_accessed=8000000, transcendentals=0),
        name="own_sums",
    )(listed, counts, blk)


def fit_kernel(sum_ref, weight_ref, h0_ref, h1_ref, h2_ref, vertex_ref, count_ref, out_ref, moment_ref, total_ref):
    sub = lax.broadcasted_iota(jnp.int32, (8, LANES), 0)
    for side, ref in enumerate((h0_ref, h1_ref, h2_ref)):
        moment_rows(sub, ref, slice(0, LANES), moment_ref, slice(side * LANES, (side + 1) * LANES))
    patches = weight_ref.shape[1]
    total_ref[...] = sum_ref[...] + summed_over(moment_ref[...], weight_ref[...], 0)

    def row(ref, start):
        return jnp.broadcast_to(ref[start:start + 1, 0:patches], (8, patches))

    def both(start):
        return row(total_ref, start) + row(total_ref, start + 4)

    points = 4.0 * row(count_ref, 0).astype(jnp.float32)
    vertex = [row(vertex_ref, dim) for dim in range(3)]
    sum_x = [both(64 + dim) for dim in range(3)]
    sum_xx = {
        (0, 0): both(72), (1, 1): both(73), (2, 2): both(74),
        (0, 1): both(80), (1, 2): both(81), (0, 2): both(88),
    }
    gram = {(0, 0): points + RIDGE}
    for a in range(3):
        gram[0, a + 1] = sum_x[a] - points * vertex[a]
        for b in range(a, 3):
            value = sum_xx[a, b] - vertex[a] * sum_x[b] - sum_x[a] * vertex[b] + points * vertex[a] * vertex[b]
            gram[a + 1, b + 1] = value + RIDGE if a == b else value
    rhs = []
    for step in range(2):
        base = total_ref[32 * step:32 * step + 8, :]
        rest = [total_ref[32 * step + 8 * dim + 8:32 * step + 8 * dim + 16, :] for dim in range(3)]
        rhs.append([base] + [rest[dim] - vertex[dim] * base for dim in range(3)])
    for pivot in (3, 2, 1):
        inverse = 1.0 / gram[pivot, pivot]
        for other in range(pivot):
            factor = gram[other, pivot] * inverse
            for column in range(other, pivot):
                gram[other, column] = gram[other, column] - factor * gram[column, pivot]
            for step in range(2):
                rhs[step][other] = rhs[step][other] - factor * rhs[step][pivot]
    inverse = 1.0 / gram[0, 0]
    for step in range(2):
        out_ref[6 * step:6 * step + 6, :] = (rhs[step][0] * inverse)[0:6]


def fit(sums, weights, halos, coords, counts):
    patches = weights.shape[1]
    return pl.pallas_call(
        fit_kernel,
        out_shape=jax.ShapeDtypeStruct((12, patches), jnp.float32),
        in_specs=[VMEM] * 7,
        out_specs=VMEM,
        scratch_shapes=[
            pltpu.VMEM((96, 3 * LANES), jnp.float32),
            pltpu.VMEM((96, patches), jnp.float32),
        ],
        compiler_params=pltpu.CompilerParams(vmem_limit_bytes=LIMIT),
        name="fit",
    )(sums, weights, *halos, coords, counts)


def exchange(to_prev, to_next, to_other):
    count = lax.axis_size("dom")
    up = [(i, (i + 1) % count) for i in range(count)]
    down = [(j, i) for i, j in up]
    swap = [(0, 1), (1, 0)]
    from_prev = lax.ppermute(to_next, "dom", up)
    from_next = lax.ppermute(to_prev, "dom", down)
    from_other = lax.ppermute(to_other, "slab", swap)
    return from_prev, from_next, from_other


def local(coords, disp, oper, conn, node_send, element_send, patch_elements, patch_count):
    node_send = node_send.transpose(1, 0, 2)
    element_send = element_send.transpose(1, 0, 2)
    oper = oper.transpose(1, 0, 2)
    listed = patch_elements.T
    far = [pltpu.with_memory_space_constraint(x, pltpu.HBM) for x in (
        coords, disp, node_send, conn, oper, listed, patch_count, element_send
    )]
    *picked, table, ninth, coords_near, conn_near = node_pick(*far[0:4])
    halos = exchange(*picked)
    first, last, oper, listed, counts, send = own_gather(
        table, ninth, conn_near, *far[4:8]
    )
    blk, *picked = make_blocks(first, last, conn_near, oper, halos, send, coords.shape[1] // LANES)
    halos = exchange(*picked)
    sums, weights = own_sums(listed, counts, blk)
    return fit(sums, weights, halos, coords_near, counts)


def solution(mesh):
    both = ("dom", "slab")
    in_specs = (
        P(None, both),
        P(None, both),
        P(None, None, both),
        P(None, both),
        P(both, None, None),
        P(both, None, None),
        P(None, both),
        P(both, None),
    )
    return jax.shard_map(local, mesh=mesh, in_specs=in_specs, out_specs=P(None, both), check_vma=False)
```

```python
import jax
import jax.numpy as jnp
import numpy as np
from jax import lax
from jax.experimental import pallas as pl
from jax.experimental.pallas import tpu as pltpu
from jax.sharding import PartitionSpec as P

RIDGE = 1.0
LANES = 128
VMEM = pl.BlockSpec(memory_space=pltpu.VMEM)
HBM = pl.BlockSpec(memory_space=pltpu.HBM)
UNROLL = 2
WIDTH = 64
EDGE = 4
LIMIT = 24 * 1024 * 1024


def shape_table():
    near = 0.5854101966249685
    far = 0.1381966011250105
    edge_pairs = ((0, 1), (1, 2), (0, 2), (0, 3), (1, 3), (2, 3))
    table_rows = []
    for corner in range(4):
        barycentric = [far, far, far, far]
        barycentric[corner] = near
        values = [b * (2.0 * b - 1.0) for b in barycentric]
        values = values + [4.0 * barycentric[a] * barycentric[b] for a, b in edge_pairs]
        table_rows.append(values)
    return np.array(table_rows, np.float32)


SHAPE = shape_table()


def lane_gather(table, index):
    return jnp.take_along_axis(table, index, axis=1, mode="promise_in_bounds")


def rows8(ref, row, lanes):
    return jnp.broadcast_to(ref[pl.ds(row, 1), lanes], (8, LANES))


def start_all(pairs, sems):
    copies = [pltpu.make_async_copy(src, dst, sems.at[k]) for k, (src, dst) in enumerate(pairs)]
    for copy in copies:
        copy.start()
    return copies


def ninth_row(sub, table, low, high, chunks):
    total = jnp.zeros((8, LANES), jnp.float32)
    for start in range(0, chunks, 8):
        piece = lane_gather(table[start:start + 8, :], low)
        total = jnp.where(high == sub + start, piece, total)
    return total


def node_pick_kernel(
    coords_hbm, disp_hbm, send_hbm, conn_hbm,
    prev_ref, next_ref, other_ref, table_ref, ninth_ref, coords_ref, conn_ref,
    disp_ref, send_ref, sems,
):
    pairs = ((coords_hbm, coords_ref), (disp_hbm, disp_ref), (send_hbm, send_ref), (conn_hbm, conn_ref))
    copies = start_all(pairs, sems)
    for copy in copies[0:3]:
        copy.wait()
    sub = lax.broadcasted_iota(jnp.int32, (8, LANES), 0)
    chunks = table_ref.shape[0]
    ninth_ref[8:16, :] = jnp.zeros((8, LANES), jnp.float32)
    for chunk in range(chunks):
        lanes = pl.ds(chunk * LANES, LANES)
        table_ref[chunk, 0:3, :] = coords_ref[:, lanes]
        table_ref[chunk, 3:8, :] = disp_ref[0:5, lanes]
        ninth_ref[chunk:chunk + 1, :] = disp_ref[5:6, lanes]
    for side, out_ref in enumerate((prev_ref, next_ref, other_ref)):
        index = jnp.broadcast_to(send_ref[side], (8, LANES))
        low, high = index & 127, index >> 7
        first = jnp.zeros((8, LANES), jnp.float32)
        for chunk in range(chunks):
            first = jnp.where(high == chunk, lane_gather(table_ref[chunk], low), first)
        out_ref[0:8, :] = first
        last = ninth_row(sub, ninth_ref, low, high, chunks)
        out_ref[8:9, :] = jnp.sum(last, axis=0, keepdims=True)
    copies[3].wait()


def node_pick(coords, disp, send, conn):
    out = jax.ShapeDtypeStruct((9, LANES), jnp.float32)
    chunks = coords.shape[1] // LANES
    return pl.pallas_call(
        node_pick_kernel,
        out_shape=(
            out, out, out,
            jax.ShapeDtypeStruct((chunks, 8, LANES), jnp.float32),
            jax.ShapeDtypeStruct((16, LANES), jnp.float32),
            jax.ShapeDtypeStruct(coords.shape, coords.dtype),
            jax.ShapeDtypeStruct(conn.shape, conn.dtype),
        ),
        in_specs=[HBM] * 4,
        out_specs=(VMEM,) * 7,
        scratch_shapes=[
            pltpu.VMEM(disp.shape, disp.dtype),
            pltpu.VMEM(send.shape, send.dtype),
            pltpu.SemaphoreType.DMA((4,)),
        ],
        compiler_params=pltpu.CompilerParams(vmem_limit_bytes=LIMIT),
        name="node_pick",
    )(coords, disp, send, conn)


def at_edge():
    return lax.rem(lax.axis_index("dom"), EDGE) == 0


def gather_work(table_ref, ninth_ref, conn_ref, far, near, sems):
    first_ref, last_ref = near[0:2]
    copies = start_all(tuple(zip(far, near[2:6])), sems)
    sub = lax.broadcasted_iota(jnp.int32, (8, LANES), 0)
    chunks = table_ref.shape[0]

    def group(block, carry):
        lanes = pl.ds(pl.multiple_of(block * LANES, LANES), LANES)
        for node in range(10):
            index = rows8(conn_ref, node, lanes)
            low, high = index & 127, index >> 7
            first = jnp.zeros((8, LANES), jnp.float32)
            for chunk in range(chunks):
                first = jnp.where(high == chunk, lane_gather(table_ref[chunk], low), first)
            first_ref[node, :, lanes] = first
            last = ninth_row(sub, ninth_ref, low, high, chunks)
            last_ref[node:node + 1, lanes] = jnp.sum(last, axis=0, keepdims=True)
        return carry

    lax.fori_loop(0, conn_ref.shape[1] // LANES, group, 0)
    for copy in copies:
        copy.wait()


def early_gather_kernel(*refs):
    held, outs, sems = refs[7:9], refs[15:17], refs[17]
    for source, target in zip(held, outs):
        target[...] = source[...]

    @pl.when(at_edge())
    def _():
        gather_work(*refs[0:3], refs[3:7], refs[9:15], sems)


def late_gather_kernel(*refs):
    sems = refs[19]
    done, near = refs[7:13], refs[13:19]

    @pl.when(at_edge())
    def _():
        for source, target in zip(done, near):
            target[...] = source[...]

    @pl.when(jnp.logical_not(at_edge()))
    def _():
        gather_work(*refs[0:3], refs[3:7], near, sems)


def own_gather(table, ninth, conn, far, held=None, done=None):
    elems = conn.shape[1]
    outs = [jax.ShapeDtypeStruct((10, 8, elems), jnp.float32), jax.ShapeDtypeStruct((10, elems), jnp.float32)]
    outs = outs + [jax.ShapeDtypeStruct(x.shape, x.dtype) for x in far]
    extra = list(done) if held is None else list(held)
    if held is not None:
        outs = outs + [jax.ShapeDtypeStruct(x.shape, x.dtype) for x in held]
    return pl.pallas_call(
        late_gather_kernel if held is None else early_gather_kernel,
        out_shape=tuple(outs),
        in_specs=[VMEM] * 3 + [HBM] * 4 + [VMEM] * len(extra),
        out_specs=(VMEM,) * len(outs),
        scratch_shapes=[pltpu.SemaphoreType.DMA((4,))],
        compiler_params=pltpu.CompilerParams(vmem_limit_bytes=LIMIT),
        cost_estimate=pl.CostEstimate(flops=20000000, bytes_accessed=4000000, transcendentals=0),
        name="late_gather" if held is None else "early_gather",
    )(table, ninth, conn, *far, *extra)


def block_kernel(
    first_halo, first_ref, last_ref, conn_ref, oper_ref, h0_ref, h1_ref, h2_ref, send_ref,
    blk_ref, prev_ref, next_ref, other_ref, ninth_ref, full_ref,
):
    halos = (h0_ref, h1_ref, h2_ref)
    for side, ref in enumerate(halos):
        ninth_ref[side:side + 1, :] = ref[8:9, :]
    sub = lax.broadcasted_iota(jnp.int32, (8, LANES), 0)
    groups = conn_ref.shape[1] // LANES

    def group(block, slot):
        lanes = pl.ds(pl.multiple_of(block * LANES, LANES), LANES)
        corners, edges = [], []
        for node in range(10):
            index = rows8(conn_ref, node, lanes)
            low, high = index & 127, index >> 7
            first = first_ref[node, :, lanes]
            for side in range(3):
                first = jnp.where(high == first_halo + side, lane_gather(halos[side][0:8, :], low), first)
            (corners if node < 4 else edges).append(first)
            full_ref[slot, node, 0:8, :] = first
            last = jnp.where(high == sub + first_halo, lane_gather(ninth_ref[...], low), 0.0)
            full_ref[slot, node, 8:16, :] = jnp.where(sub == 3, rows8(last_ref, node, lanes), last)
        totals = [[jnp.zeros((8, LANES), jnp.float32) for _ in range(3)] for _ in range(2)]
        for node in range(10):
            for comp in range(3):
                oper = oper_ref[3 * node + comp, :, lanes].astype(jnp.float32)
                for step in range(2):
                    row = 3 + 3 * step + comp
                    value = jnp.broadcast_to(full_ref[slot, node, row:row + 1, :], (8, LANES))
                    if row == 8:
                        for extra in (9, 10, 11):
                            value = value + jnp.broadcast_to(full_ref[slot, node, extra:extra + 1, :], (8, LANES))
                    for part in range(3):
                        totals[step][part] = totals[step][part] + oper[8 * part:8 * part + 8] * value
        for step in range(2):
            for part in range(3):
                row = 24 * step + 8 * part
                blk_ref[row:row + 8, lanes] = totals[step][part]
        points = []
        for quad in range(4):
            total = corners[0] * SHAPE[quad, 0]
            for node in range(1, 10):
                total = total + (corners + edges)[node] * SHAPE[quad, node]
            points.append(total)
        blk_ref[48:56, lanes] = jnp.where(sub < 4, points[0], pltpu.roll(points[1], 4, 0))
        blk_ref[56:64, lanes] = jnp.where(sub < 4, points[2], pltpu.roll(points[3], 4, 0))

    def pair(block, carry):
        for slot in range(UNROLL):
            group(block * UNROLL + slot, slot)
        return carry

    lax.fori_loop(0, groups // UNROLL, pair, 0)
    for side, out_ref in enumerate((prev_ref, next_ref, other_ref)):
        index = jnp.broadcast_to(send_ref[side], (8, LANES))
        low, high = index & 127, index >> 7
        hits = [high == chunk for chunk in range(groups)]
        for row in range(0, 64, 8):
            total = jnp.zeros((8, LANES), jnp.float32)
            for chunk in range(groups):
                piece = blk_ref[row:row + 8, chunk * LANES:(chunk + 1) * LANES]
                total = jnp.where(hits[chunk], lane_gather(piece, low), total)
            out_ref[row:row + 8, :] = total


def make_blocks(first, last, conn, oper, halos, send, first_halo):
    elems = conn.shape[1]
    out = jax.ShapeDtypeStruct((64, LANES), jnp.float32)

    def kernel(*refs):
        block_kernel(first_halo, *refs)

    return pl.pallas_call(
        kernel,
        out_shape=(jax.ShapeDtypeStruct((64, elems), jnp.float32), out, out, out),
        in_specs=[VMEM] * 8,
        out_specs=(VMEM,) * 4,
        scratch_shapes=[
            pltpu.VMEM((8, LANES), jnp.float32),
            pltpu.VMEM((UNROLL, 10, 16, LANES), jnp.float32),
        ],
        compiler_params=pltpu.CompilerParams(vmem_limit_bytes=LIMIT),
        name="make_blocks",
    )(first, last, conn, oper, *halos, send)


def add_points(sub, piece):
    pair = jnp.where(sub >= 6, piece[0], piece[1])
    later = jnp.where(sub >= 4, piece[1], piece[2])
    return piece[0] + pltpu.roll(pair, 2, 0) + pltpu.roll(later, 4, 0) + pltpu.roll(piece[2], 6, 0)


def moment_rows(sub, ref, lanes, out_ref, out_lanes):
    spread = []
    for dim in range(3):
        rows = [rows8(ref, 48 + 4 * quad + dim, lanes) for quad in range(4)]
        spread.append([jnp.where(sub < 6 - 2 * k, rows[k], rows[k + 1]) for k in range(3)])
    for step in range(2):
        piece = [ref[24 * step + 8 * k:24 * step + 8 * k + 8, lanes] for k in range(3)]
        base = 32 * step
        out_ref[base:base + 8, out_lanes] = add_points(sub, piece)
        for dim in range(3):
            scaled = [piece[k] * spread[dim][k] for k in range(3)]
            out_ref[base + 8 * dim + 8:base + 8 * dim + 16, out_lanes] = add_points(sub, scaled)
    pair = [ref[48:56, lanes], ref[56:64, lanes]]
    out_ref[64:72, out_lanes] = pair[0] + pair[1]
    out_ref[72:80, out_lanes] = pair[0] * pair[0] + pair[1] * pair[1]
    for shift in (1, 2):
        total = pair[0] * pltpu.roll(pair[0], 8 - shift, 0) + pair[1] * pltpu.roll(pair[1], 8 - shift, 0)
        out_ref[72 + 8 * shift:80 + 8 * shift, out_lanes] = total


def summed_over(moments, weights, weight_dim):
    total = None
    rest = moments
    for part in range(3):
        piece = rest.astype(jnp.bfloat16)
        if part < 2:
            rest = rest - piece.astype(jnp.float32)
        term = lax.dot_general(
            piece, weights, (((1,), (weight_dim,)), ((), ())), preferred_element_type=jnp.float32
        )
        total = term if total is None else total + term
    return total


def sum_work(
    list_ref, count_ref, blk_ref, sum_ref, halo_ref, index_ref, hist_ref, weight_ref, moment_ref
):
    patches, slots = list_ref.shape
    counts = count_ref[...].astype(jnp.float32)
    diagonal = lax.broadcasted_iota(jnp.int32, (patches, patches), 0) == lax.broadcasted_iota(
        jnp.int32, (patches, patches), 1
    )
    spread = jnp.where(diagonal, jnp.broadcast_to(counts, (patches, patches)), 0.0)
    limits = jnp.dot(
        spread.astype(jnp.bfloat16),
        jnp.ones((patches, slots), jnp.bfloat16),
        preferred_element_type=jnp.float32,
    ).astype(jnp.int32)
    slot = lax.broadcasted_iota(jnp.int32, (patches, slots), 1)
    index_ref[...] = jnp.where(slot < limits, list_ref[...], 4095)
    low_ids = lax.broadcasted_iota(jnp.int32, (LANES, slots), 0)
    high_ids = lax.broadcasted_iota(jnp.int32, (16, slots), 0)
    width = WIDTH

    def group(block, carry):
        start = pl.multiple_of(block * width, width)
        listed = index_ref[pl.ds(start, width), :]
        low, high = listed & 127, listed >> 7
        for patch in range(width):
            low_hit = low_ids == jnp.broadcast_to(low[patch:patch + 1], (LANES, slots))
            high_hit = high_ids == jnp.broadcast_to(high[patch:patch + 1], (16, slots))
            hist = lax.dot_general(
                jnp.where(high_hit, 1.0, 0.0).astype(jnp.float8_e4m3fn),
                jnp.where(low_hit, 1.0, 0.0).astype(jnp.float8_e4m3fn),
                (((1,), (1,)), ((), ())),
                preferred_element_type=jnp.float32,
            )
            hist_ref[pl.ds(pl.multiple_of(start * 16, LANES) + 16 * patch, 16), :] = hist
        return carry

    lax.fori_loop(0, patches // width, group, 0)
    elems = blk_ref.shape[1]
    chunks = elems // LANES
    for chunk in range(chunks + 3):
        column = hist_ref[pl.ds(chunk, patches, stride=16), :]
        if chunk < chunks:
            weight_ref[:, chunk * LANES:(chunk + 1) * LANES] = column.astype(jnp.bfloat16)
        else:
            row = (chunk - chunks) * LANES
            halo_ref[row:row + LANES, :] = column.T.astype(jnp.bfloat16)
    sub = lax.broadcasted_iota(jnp.int32, (8, LANES), 0)

    def moments(block, carry):
        lanes = pl.ds(pl.multiple_of(block * LANES, LANES), LANES)
        moment_rows(sub, blk_ref, lanes, moment_ref, lanes)
        return carry

    lax.fori_loop(0, chunks, moments, 0)
    sum_ref[...] = summed_over(moment_ref[...], weight_ref[...], 1)


def early_sum_kernel(
    list_ref, count_ref, blk_ref, prev_ref, other_ref, sum_ref, halo_ref, prev_out, other_out, *scratch
):
    prev_out[...] = prev_ref[...]
    other_out[...] = other_ref[...]

    @pl.when(at_edge())
    def _():
        sum_work(list_ref, count_ref, blk_ref, sum_ref, halo_ref, *scratch)


def late_sum_kernel(list_ref, count_ref, blk_ref, sum_in, halo_in, sum_ref, halo_ref, *scratch):
    @pl.when(at_edge())
    def _():
        sum_ref[...] = sum_in[...]
        halo_ref[...] = halo_in[...]

    @pl.when(jnp.logical_not(at_edge()))
    def _():
        sum_work(list_ref, count_ref, blk_ref, sum_ref, halo_ref, *scratch)


def own_sums(listed, counts, blk, held=None, done=None):
    patches, slots = listed.shape
    elems = blk.shape[1]
    outs = [
        jax.ShapeDtypeStruct((96, patches), jnp.float32),
        jax.ShapeDtypeStruct((3 * LANES, patches), jnp.bfloat16),
    ]
    extra = list(done) if held is None else list(held)
    if held is not None:
        outs = outs + [jax.ShapeDtypeStruct(x.shape, x.dtype) for x in held]
    return pl.pallas_call(
        late_sum_kernel if held is None else early_sum_kernel,
        out_shape=tuple(outs),
        in_specs=[VMEM] * (3 + len(extra)),
        out_specs=(VMEM,) * len(outs),
        scratch_shapes=[
            pltpu.VMEM((patches, slots), jnp.int32),
            pltpu.VMEM((patches * 16, LANES), jnp.float32),
            pltpu.VMEM((patches, elems), jnp.bfloat16),
            pltpu.VMEM((96, elems), jnp.float32),
        ],
        compiler_params=pltpu.CompilerParams(vmem_limit_bytes=LIMIT),
        cost_estimate=pl.CostEstimate(flops=40000000, bytes_accessed=8000000, transcendentals=0),
        name="late_sums" if held is None else "early_sums",
    )(listed, counts, blk, *extra)


def fit_kernel(sum_ref, weight_ref, h0_ref, h1_ref, h2_ref, vertex_ref, count_ref, out_ref, moment_ref, total_ref):
    sub = lax.broadcasted_iota(jnp.int32, (8, LANES), 0)
    for side, ref in enumerate((h0_ref, h1_ref, h2_ref)):
        moment_rows(sub, ref, slice(0, LANES), moment_ref, slice(side * LANES, (side + 1) * LANES))
    patches = weight_ref.shape[1]
    total_ref[...] = sum_ref[...] + summed_over(moment_ref[...], weight_ref[...], 0)

    def row(ref, start):
        return jnp.broadcast_to(ref[start:start + 1, 0:patches], (8, patches))

    def both(start):
        return row(total_ref, start) + row(total_ref, start + 4)

    points = 4.0 * row(count_ref, 0).astype(jnp.float32)
    vertex = [row(vertex_ref, dim) for dim in range(3)]
    sum_x = [both(64 + dim) for dim in range(3)]
    sum_xx = {
        (0, 0): both(72), (1, 1): both(73), (2, 2): both(74),
        (0, 1): both(80), (1, 2): both(81), (0, 2): both(88),
    }
    gram = {(0, 0): points + RIDGE}
    for a in range(3):
        gram[0, a + 1] = sum_x[a] - points * vertex[a]
        for b in range(a, 3):
            value = sum_xx[a, b] - vertex[a] * sum_x[b] - sum_x[a] * vertex[b] + points * vertex[a] * vertex[b]
            gram[a + 1, b + 1] = value + RIDGE if a == b else value
    rhs = []
    for step in range(2):
        base = total_ref[32 * step:32 * step + 8, :]
        rest = [total_ref[32 * step + 8 * dim + 8:32 * step + 8 * dim + 16, :] for dim in range(3)]
        rhs.append([base] + [rest[dim] - vertex[dim] * base for dim in range(3)])
    for pivot in (3, 2, 1):
        inverse = 1.0 / gram[pivot, pivot]
        for other in range(pivot):
            factor = gram[other, pivot] * inverse
            for column in range(other, pivot):
                gram[other, column] = gram[other, column] - factor * gram[column, pivot]
            for step in range(2):
                rhs[step][other] = rhs[step][other] - factor * rhs[step][pivot]
    inverse = 1.0 / gram[0, 0]
    for step in range(2):
        out_ref[6 * step:6 * step + 6, :] = (rhs[step][0] * inverse)[0:6]


def fit(sums, weights, halos, coords, counts):
    patches = weights.shape[1]
    return pl.pallas_call(
        fit_kernel,
        out_shape=jax.ShapeDtypeStruct((12, patches), jnp.float32),
        in_specs=[VMEM] * 7,
        out_specs=VMEM,
        scratch_shapes=[
            pltpu.VMEM((96, 3 * LANES), jnp.float32),
            pltpu.VMEM((96, patches), jnp.float32),
        ],
        compiler_params=pltpu.CompilerParams(vmem_limit_bytes=LIMIT),
        name="fit",
    )(sums, weights, *halos, coords, counts)


def exchange(to_prev, to_next, to_other, early):
    count = lax.axis_size("dom")
    up = [(i, (i + 1) % count) for i in range(count)]
    down = [(j, i) for i, j in up]
    swap = [(0, 1), (1, 0)]
    from_prev = lax.ppermute(to_next, "dom", up)
    *done, to_prev, to_other = early((to_prev, to_other))
    from_next = lax.ppermute(to_prev, "dom", down)
    from_other = lax.ppermute(to_other, "slab", swap)
    return (from_prev, from_next, from_other), done


def local(coords, disp, oper, conn, node_send, element_send, patch_elements, patch_count):
    node_send = node_send.transpose(1, 0, 2)
    element_send = element_send.transpose(1, 0, 2)
    oper = oper.transpose(1, 0, 2)
    listed = patch_elements.T
    far = [pltpu.with_memory_space_constraint(x, pltpu.HBM) for x in (
        coords, disp, node_send, conn, oper, listed, patch_count, element_send
    )]
    *picked, table, ninth, coords_near, conn_near = node_pick(*far[0:4])
    own = (table, ninth, conn_near, far[4:8])
    halos, done = exchange(*picked, lambda held: own_gather(*own, held=held))
    first, last, oper, listed, counts, send = own_gather(*own, done=done)
    blk, *picked = make_blocks(first, last, conn_near, oper, halos, send, coords.shape[1] // LANES)
    own = (listed, counts, blk)
    halos, done = exchange(*picked, lambda held: own_sums(*own, held=held))
    sums, weights = own_sums(*own, done=done)
    return fit(sums, weights, halos, coords_near, counts)


def solution(mesh):
    both = ("dom", "slab")
    in_specs = (
        P(None, both),
        P(None, both),
        P(None, None, both),
        P(None, both),
        P(both, None, None),
        P(both, None, None),
        P(None, both),
        P(both, None),
    )
    return jax.shard_map(local, mesh=mesh, in_specs=in_specs, out_specs=P(None, both), check_vma=False)
```

```python
import jax
import jax.numpy as jnp
import numpy as np
from jax import lax
from jax.experimental import pallas as pl
from jax.experimental.pallas import tpu as pltpu
from jax.sharding import PartitionSpec as P

RIDGE = 1.0
LANES = 128
VMEM = pl.BlockSpec(memory_space=pltpu.VMEM)
HBM = pl.BlockSpec(memory_space=pltpu.HBM)
WIDTH = 64
EDGE = 4
SUM_REACH = 2
LIMIT = 24 * 1024 * 1024


EDGES = ((0, 1), (1, 2), (0, 2), (0, 3), (1, 3), (2, 3))


def shape_table():
    near = 0.5854101966249685
    far = 0.1381966011250105
    table_rows = []
    for corner in range(4):
        barycentric = [far, far, far, far]
        barycentric[corner] = near
        values = [b * (2.0 * b - 1.0) for b in barycentric]
        values = values + [4.0 * barycentric[a] * barycentric[b] for a, b in EDGES]
        table_rows.append(values)
    return np.array(table_rows, np.float32)


SHAPE = shape_table()


def lane_gather(table, index):
    return jnp.take_along_axis(table, index, axis=1, mode="promise_in_bounds")


def rows8(ref, row, lanes):
    return jnp.broadcast_to(ref[pl.ds(row, 1), lanes], (8, LANES))


def start_all(pairs, sems):
    copies = [pltpu.make_async_copy(src, dst, sems.at[k]) for k, (src, dst) in enumerate(pairs)]
    for copy in copies:
        copy.start()
    return copies


def ninth_row(sub, table, low, high, chunks):
    total = jnp.zeros((8, LANES), jnp.float32)
    for start in range(0, chunks, 8):
        piece = lane_gather(table[start:start + 8, :], low)
        total = jnp.where(high == sub + start, piece, total)
    return total


def node_pick_kernel(
    coords_hbm, disp_hbm, send_hbm, conn_hbm,
    prev_ref, next_ref, other_ref, table_ref, ninth_ref, coords_ref, conn_ref,
    disp_ref, send_ref, sems,
):
    pairs = ((coords_hbm, coords_ref), (disp_hbm, disp_ref), (send_hbm, send_ref), (conn_hbm, conn_ref))
    copies = start_all(pairs, sems)
    for copy in copies[0:3]:
        copy.wait()
    sub = lax.broadcasted_iota(jnp.int32, (8, LANES), 0)
    chunks = table_ref.shape[0]
    ninth_ref[8:16, :] = jnp.zeros((8, LANES), jnp.float32)
    for chunk in range(chunks):
        lanes = pl.ds(chunk * LANES, LANES)
        table_ref[chunk, 0:3, :] = coords_ref[:, lanes]
        table_ref[chunk, 3:8, :] = disp_ref[0:5, lanes]
        ninth_ref[chunk:chunk + 1, :] = disp_ref[5:6, lanes]
    for side, out_ref in enumerate((prev_ref, next_ref, other_ref)):
        index = jnp.broadcast_to(send_ref[side], (8, LANES))
        low, high = index & 127, index >> 7
        first = jnp.zeros((8, LANES), jnp.float32)
        for chunk in range(chunks):
            first = jnp.where(high == chunk, lane_gather(table_ref[chunk], low), first)
        out_ref[0:8, :] = first
        last = ninth_row(sub, ninth_ref, low, high, chunks)
        out_ref[8:9, :] = jnp.sum(last, axis=0, keepdims=True)
    copies[3].wait()


def node_pick(coords, disp, send, conn):
    out = jax.ShapeDtypeStruct((9, LANES), jnp.float32)
    chunks = coords.shape[1] // LANES
    return pl.pallas_call(
        node_pick_kernel,
        out_shape=(
            out, out, out,
            jax.ShapeDtypeStruct((chunks, 8, LANES), jnp.float32),
            jax.ShapeDtypeStruct((16, LANES), jnp.float32),
            jax.ShapeDtypeStruct(coords.shape, coords.dtype),
            jax.ShapeDtypeStruct(conn.shape, conn.dtype),
        ),
        in_specs=[HBM] * 4,
        out_specs=(VMEM,) * 7,
        scratch_shapes=[
            pltpu.VMEM(disp.shape, disp.dtype),
            pltpu.VMEM(send.shape, send.dtype),
            pltpu.SemaphoreType.DMA((4,)),
        ],
        compiler_params=pltpu.CompilerParams(vmem_limit_bytes=LIMIT),
        name="node_pick",
    )(coords, disp, send, conn)


def near_edge(reach):
    return lax.rem(lax.axis_index("dom"), EDGE) < reach


def gather_work(table_ref, ninth_ref, conn_ref, far, near, sems):
    first_ref, last_ref = near[0:2]
    copies = start_all(tuple(zip(far, near[2:6])), sems)
    sub = lax.broadcasted_iota(jnp.int32, (8, LANES), 0)
    chunks = table_ref.shape[0]

    def group(block, carry):
        lanes = pl.ds(pl.multiple_of(block * LANES, LANES), LANES)
        for node in range(10):
            index = rows8(conn_ref, node, lanes)
            low, high = index & 127, index >> 7
            first = jnp.zeros((8, LANES), jnp.float32)
            for chunk in range(chunks):
                first = jnp.where(high == chunk, lane_gather(table_ref[chunk], low), first)
            first_ref[node, :, lanes] = first
            last = ninth_row(sub, ninth_ref, low, high, chunks)
            last_ref[node:node + 1, lanes] = jnp.sum(last, axis=0, keepdims=True)
        return carry

    lax.fori_loop(0, conn_ref.shape[1] // LANES, group, 0)
    for copy in copies:
        copy.wait()


def early_gather_kernel(*refs):
    count = (len(refs) - 14) // 2
    held, sems = refs[7:7 + count], refs[-1]
    near, outs = refs[7 + count:13 + count], refs[13 + count:13 + 2 * count]
    for source, target in zip(held, outs):
        target[...] = source[...]

    @pl.when(near_edge(1))
    def _():
        gather_work(*refs[0:3], refs[3:7], near, sems)


def late_gather_kernel(*refs):
    sems = refs[19]
    done, near = refs[7:13], refs[13:19]

    @pl.when(near_edge(1))
    def _():
        for source, target in zip(done, near):
            target[...] = source[...]

    @pl.when(jnp.logical_not(near_edge(1)))
    def _():
        gather_work(*refs[0:3], refs[3:7], near, sems)


def own_gather(table, ninth, conn, far, held=None, done=None):
    elems = conn.shape[1]
    outs = [jax.ShapeDtypeStruct((10, 8, elems), jnp.float32), jax.ShapeDtypeStruct((10, elems), jnp.float32)]
    outs = outs + [jax.ShapeDtypeStruct(x.shape, x.dtype) for x in far]
    extra = list(done) if held is None else list(held)
    if held is not None:
        outs = outs + [jax.ShapeDtypeStruct(x.shape, x.dtype) for x in held]
    return pl.pallas_call(
        late_gather_kernel if held is None else early_gather_kernel,
        out_shape=tuple(outs),
        in_specs=[VMEM] * 3 + [HBM] * 4 + [VMEM] * len(extra),
        out_specs=(VMEM,) * len(outs),
        scratch_shapes=[pltpu.SemaphoreType.DMA((4,))],
        compiler_params=pltpu.CompilerParams(vmem_limit_bytes=LIMIT),
        cost_estimate=pl.CostEstimate(flops=20000000, bytes_accessed=4000000, transcendentals=0),
        name="late_gather" if held is None else "early_gather",
    )(table, ninth, conn, *far, *extra)


def block_kernel(
    first_halo, first_ref, last_ref, conn_ref, oper_ref, h0_ref, h1_ref, h2_ref, send_ref,
    blk_ref, prev_ref, next_ref, other_ref, ninth_ref, full_ref,
):
    halos = (h0_ref, h1_ref, h2_ref)
    for side, ref in enumerate(halos):
        ninth_ref[side:side + 1, :] = ref[8:9, :]
    sub = lax.broadcasted_iota(jnp.int32, (8, LANES), 0)
    groups = conn_ref.shape[1] // LANES
    ends = SHAPE[0, 1], SHAPE[0, 0] - SHAPE[0, 1]
    mids = SHAPE[0, 5], SHAPE[0, 4] - SHAPE[0, 5]

    def group(block):
        lanes = slice(block * LANES, (block + 1) * LANES)
        nodes = []
        for node in range(10):
            index = rows8(conn_ref, node, lanes)
            low, high = index & 127, index >> 7
            first = first_ref[node, :, lanes]
            for side in range(3):
                first = jnp.where(high == first_halo + side, lane_gather(halos[side][0:8, :], low), first)
            nodes.append(first)
            full_ref[block, node, 0:8, :] = first
            last = jnp.where(high == sub + first_halo, lane_gather(ninth_ref[...], low), 0.0)
            full_ref[block, node, 8:16, :] = last
        totals = [[None] * 3 for _ in range(2)]
        for node in range(10):
            for comp in range(3):
                oper = oper_ref[3 * node + comp, :, lanes].astype(jnp.float32)
                for step in range(2):
                    row = 3 + 3 * step + comp
                    value = rows8(full_ref.at[block, node], row, slice(0, LANES))
                    if row == 8:
                        value = value + rows8(last_ref, node, lanes)
                        for extra in (9, 10):
                            value = value + rows8(full_ref.at[block, node], extra, slice(0, LANES))
                    for part in range(3):
                        term = oper[8 * part:8 * part + 8] * value
                        total = totals[step][part]
                        totals[step][part] = term if total is None else total + term
        pieces = totals[0] + totals[1]
        shared = (nodes[0] + nodes[1] + nodes[2] + nodes[3]) * ends[0] + (
            nodes[4] + nodes[5] + nodes[6] + nodes[7] + nodes[8] + nodes[9]
        ) * mids[0]
        points = []
        for quad in range(4):
            a, b, c = [4 + k for k, pair in enumerate(EDGES) if quad in pair]
            points.append(shared + nodes[quad] * ends[1] + (nodes[a] + nodes[b] + nodes[c]) * mids[1])
        pieces.append(jnp.where(sub < 4, points[0], pltpu.roll(points[1], 4, 0)))
        pieces.append(jnp.where(sub < 4, points[2], pltpu.roll(points[3], 4, 0)))
        for part, piece in enumerate(pieces):
            blk_ref[8 * part:8 * part + 8, lanes] = piece

    for block in range(groups):
        group(block)
    for side, out_ref in enumerate((prev_ref, next_ref, other_ref)):
        index = jnp.broadcast_to(send_ref[side], (8, LANES))
        low, high = index & 127, index >> 7
        hits = [high == chunk for chunk in range(groups)]
        for row in range(0, 64, 8):
            total = jnp.zeros((8, LANES), jnp.float32)
            for chunk in range(groups):
                piece = blk_ref[row:row + 8, chunk * LANES:(chunk + 1) * LANES]
                total = jnp.where(hits[chunk], lane_gather(piece, low), total)
            out_ref[row:row + 8, :] = total


def make_blocks(first, last, conn, oper, halos, send, first_halo):
    elems = conn.shape[1]
    out = jax.ShapeDtypeStruct((64, LANES), jnp.float32)

    def kernel(*refs):
        block_kernel(first_halo, *refs)

    return pl.pallas_call(
        kernel,
        out_shape=(jax.ShapeDtypeStruct((64, elems), jnp.float32), out, out, out),
        in_specs=[VMEM] * 8,
        out_specs=(VMEM,) * 4,
        scratch_shapes=[
            pltpu.VMEM((8, LANES), jnp.float32),
            pltpu.VMEM((elems // LANES, 10, 16, LANES), jnp.float32),
        ],
        compiler_params=pltpu.CompilerParams(vmem_limit_bytes=LIMIT),
        name="make_blocks",
    )(first, last, conn, oper, *halos, send)


def add_points(sub, piece):
    pair = jnp.where(sub >= 6, piece[0], piece[1])
    later = jnp.where(sub >= 4, piece[1], piece[2])
    return piece[0] + pltpu.roll(pair, 2, 0) + pltpu.roll(later, 4, 0) + pltpu.roll(piece[2], 6, 0)


def moment_rows(sub, ref, lanes, out_ref, out_lanes):
    spread = []
    for dim in range(3):
        rows = [rows8(ref, 48 + 4 * quad + dim, lanes) for quad in range(4)]
        spread.append([jnp.where(sub < 6 - 2 * k, rows[k], rows[k + 1]) for k in range(3)])
    for step in range(2):
        piece = [ref[24 * step + 8 * k:24 * step + 8 * k + 8, lanes] for k in range(3)]
        base = 32 * step
        out_ref[base:base + 8, out_lanes] = add_points(sub, piece)
        for dim in range(3):
            scaled = [piece[k] * spread[dim][k] for k in range(3)]
            out_ref[base + 8 * dim + 8:base + 8 * dim + 16, out_lanes] = add_points(sub, scaled)
    pair = [ref[48:56, lanes], ref[56:64, lanes]]
    out_ref[64:72, out_lanes] = pair[0] + pair[1]
    out_ref[72:80, out_lanes] = pair[0] * pair[0] + pair[1] * pair[1]
    for shift in (1, 2):
        total = pair[0] * pltpu.roll(pair[0], 8 - shift, 0) + pair[1] * pltpu.roll(pair[1], 8 - shift, 0)
        out_ref[72 + 8 * shift:80 + 8 * shift, out_lanes] = total


def summed_over(moments, weights, weight_dim):
    rows = moments.shape[0]
    pieces, rest = [], moments
    for part in range(3):
        pieces.append(rest.astype(jnp.bfloat16))
        if part < 2:
            rest = rest - pieces[part].astype(jnp.float32)
    total = lax.dot_general(
        jnp.concatenate(pieces, axis=0), weights, (((1,), (weight_dim,)), ((), ())),
        preferred_element_type=jnp.float32,
    )
    return (total[2 * rows:] + total[rows:2 * rows]) + total[0:rows]


def sum_work(
    list_ref, count_ref, blk_ref, sum_ref, halo_ref, index_ref, hist_ref, weight_ref, moment_ref
):
    patches, slots = list_ref.shape
    counts = count_ref[...].astype(jnp.float32)
    diagonal = lax.broadcasted_iota(jnp.int32, (patches, patches), 0) == lax.broadcasted_iota(
        jnp.int32, (patches, patches), 1
    )
    spread = jnp.where(diagonal, jnp.broadcast_to(counts, (patches, patches)), 0.0)
    limits = jnp.dot(
        spread.astype(jnp.bfloat16),
        jnp.ones((patches, slots), jnp.bfloat16),
        preferred_element_type=jnp.float32,
    ).astype(jnp.int32)
    slot = lax.broadcasted_iota(jnp.int32, (patches, slots), 1)
    index_ref[...] = jnp.where(slot < limits, list_ref[...], 4095)
    low_ids = lax.broadcasted_iota(jnp.int32, (LANES, slots), 0)
    high_ids = lax.broadcasted_iota(jnp.int32, (16, slots), 0)
    width = WIDTH

    def group(block, carry):
        start = pl.multiple_of(block * width, width)
        listed = index_ref[pl.ds(start, width), :]
        low, high = listed & 127, listed >> 7
        for patch in range(width):
            low_hit = low_ids == jnp.broadcast_to(low[patch:patch + 1], (LANES, slots))
            high_hit = high_ids == jnp.broadcast_to(high[patch:patch + 1], (16, slots))
            hist = lax.dot_general(
                jnp.where(high_hit, 1.0, 0.0).astype(jnp.float8_e4m3fn),
                jnp.where(low_hit, 1.0, 0.0).astype(jnp.float8_e4m3fn),
                (((1,), (1,)), ((), ())),
                preferred_element_type=jnp.float32,
            )
            hist_ref[pl.ds(pl.multiple_of(start * 16, LANES) + 16 * patch, 16), :] = hist
        return carry

    lax.fori_loop(0, patches // width, group, 0)
    elems = blk_ref.shape[1]
    chunks = elems // LANES
    for chunk in range(chunks + 3):
        column = hist_ref[pl.ds(chunk, patches, stride=16), :]
        if chunk < chunks:
            weight_ref[:, chunk * LANES:(chunk + 1) * LANES] = column.astype(jnp.bfloat16)
        else:
            row = (chunk - chunks) * LANES
            halo_ref[row:row + LANES, :] = column.T.astype(jnp.bfloat16)
    sub = lax.broadcasted_iota(jnp.int32, (8, LANES), 0)

    def moments(block, carry):
        lanes = pl.ds(pl.multiple_of(block * LANES, LANES), LANES)
        moment_rows(sub, blk_ref, lanes, moment_ref, lanes)
        return carry

    lax.fori_loop(0, chunks, moments, 0)
    sum_ref[...] = summed_over(moment_ref[...], weight_ref[...], 1)


def early_sum_kernel(list_ref, count_ref, blk_ref, *refs):
    count = (len(refs) - 6) // 2
    sum_ref, halo_ref = refs[count:count + 2]
    scratch = refs[2 + 2 * count:]
    for source, target in zip(refs[0:count], refs[count + 2:2 * count + 2]):
        target[...] = source[...]

    @pl.when(near_edge(SUM_REACH))
    def _():
        sum_work(list_ref, count_ref, blk_ref, sum_ref, halo_ref, *scratch)


def late_sum_kernel(list_ref, count_ref, blk_ref, sum_in, halo_in, sum_ref, halo_ref, *scratch):
    @pl.when(near_edge(SUM_REACH))
    def _():
        sum_ref[...] = sum_in[...]
        halo_ref[...] = halo_in[...]

    @pl.when(jnp.logical_not(near_edge(SUM_REACH)))
    def _():
        sum_work(list_ref, count_ref, blk_ref, sum_ref, halo_ref, *scratch)


def own_sums(listed, counts, blk, held=None, done=None):
    patches, slots = listed.shape
    elems = blk.shape[1]
    outs = [
        jax.ShapeDtypeStruct((96, patches), jnp.float32),
        jax.ShapeDtypeStruct((3 * LANES, patches), jnp.bfloat16),
    ]
    extra = list(done) if held is None else list(held)
    if held is not None:
        outs = outs + [jax.ShapeDtypeStruct(x.shape, x.dtype) for x in held]
    return pl.pallas_call(
        late_sum_kernel if held is None else early_sum_kernel,
        out_shape=tuple(outs),
        in_specs=[VMEM] * (3 + len(extra)),
        out_specs=(VMEM,) * len(outs),
        scratch_shapes=[
            pltpu.VMEM((patches, slots), jnp.int32),
            pltpu.VMEM((patches * 16, LANES), jnp.float32),
            pltpu.VMEM((patches, elems), jnp.bfloat16),
            pltpu.VMEM((96, elems), jnp.float32),
        ],
        compiler_params=pltpu.CompilerParams(vmem_limit_bytes=LIMIT),
        cost_estimate=pl.CostEstimate(flops=40000000, bytes_accessed=8000000, transcendentals=0),
        name="late_sums" if held is None else "early_sums",
    )(listed, counts, blk, *extra)


def fit_kernel(sum_ref, weight_ref, h0_ref, h1_ref, h2_ref, vertex_ref, count_ref, out_ref, moment_ref, total_ref):
    sub = lax.broadcasted_iota(jnp.int32, (8, LANES), 0)
    for side, ref in enumerate((h0_ref, h1_ref, h2_ref)):
        moment_rows(sub, ref, slice(0, LANES), moment_ref, slice(side * LANES, (side + 1) * LANES))
    patches = weight_ref.shape[1]
    total_ref[...] = sum_ref[...] + summed_over(moment_ref[...], weight_ref[...], 0)

    def row(ref, start):
        return jnp.broadcast_to(ref[start:start + 1, 0:patches], (8, patches))

    def both(start):
        return row(total_ref, start) + row(total_ref, start + 4)

    points = 4.0 * row(count_ref, 0).astype(jnp.float32)
    vertex = [row(vertex_ref, dim) for dim in range(3)]
    sum_x = [both(64 + dim) for dim in range(3)]
    sum_xx = {
        (0, 0): both(72), (1, 1): both(73), (2, 2): both(74),
        (0, 1): both(80), (1, 2): both(81), (0, 2): both(88),
    }
    gram = {(0, 0): points + RIDGE}
    for a in range(3):
        gram[0, a + 1] = sum_x[a] - points * vertex[a]
        for b in range(a, 3):
            value = sum_xx[a, b] - vertex[a] * sum_x[b] - sum_x[a] * vertex[b] + points * vertex[a] * vertex[b]
            gram[a + 1, b + 1] = value + RIDGE if a == b else value
    rhs = []
    for step in range(2):
        base = total_ref[32 * step:32 * step + 8, :]
        rest = [total_ref[32 * step + 8 * dim + 8:32 * step + 8 * dim + 16, :] for dim in range(3)]
        rhs.append([base] + [rest[dim] - vertex[dim] * base for dim in range(3)])
    for pivot in (3, 2, 1):
        inverse = 1.0 / gram[pivot, pivot]
        for other in range(pivot):
            factor = gram[other, pivot] * inverse
            for column in range(other, pivot):
                gram[other, column] = gram[other, column] - factor * gram[column, pivot]
            for step in range(2):
                rhs[step][other] = rhs[step][other] - factor * rhs[step][pivot]
    inverse = 1.0 / gram[0, 0]
    for step in range(2):
        out_ref[6 * step:6 * step + 6, :] = (rhs[step][0] * inverse)[0:6]


def fit(sums, weights, halos, coords, counts):
    patches = weights.shape[1]
    return pl.pallas_call(
        fit_kernel,
        out_shape=jax.ShapeDtypeStruct((12, patches), jnp.float32),
        in_specs=[VMEM] * 7,
        out_specs=VMEM,
        scratch_shapes=[
            pltpu.VMEM((96, 3 * LANES), jnp.float32),
            pltpu.VMEM((96, patches), jnp.float32),
        ],
        compiler_params=pltpu.CompilerParams(vmem_limit_bytes=LIMIT),
        name="fit",
    )(sums, weights, *halos, coords, counts)


def exchange(to_prev, to_next, to_other, early):
    count = lax.axis_size("dom")
    up = [(i, (i + 1) % count) for i in range(count)]
    down = [(j, i) for i, j in up]
    swap = [(0, 1), (1, 0)]
    from_prev = lax.ppermute(to_next, "dom", up)
    *done, to_prev, to_other = early((to_prev, to_other))
    from_next = lax.ppermute(to_prev, "dom", down)
    from_other = lax.ppermute(to_other, "slab", swap)
    return (from_prev, from_next, from_other), done


def local(coords, disp, oper, conn, node_send, element_send, patch_elements, patch_count):
    node_send = node_send.transpose(1, 0, 2)
    element_send = element_send.transpose(1, 0, 2)
    oper = oper.transpose(1, 0, 2)
    listed = patch_elements.T
    far = [pltpu.with_memory_space_constraint(x, pltpu.HBM) for x in (
        coords, disp, node_send, conn, oper, listed, patch_count, element_send
    )]
    *picked, table, ninth, coords_near, conn_near = node_pick(*far[0:4])
    own = (table, ninth, conn_near, far[4:8])
    halos, done = exchange(*picked, lambda held: own_gather(*own, held=held))
    first, last, oper, listed, counts, send = own_gather(*own, done=done)
    blk, *picked = make_blocks(first, last, conn_near, oper, halos, send, coords.shape[1] // LANES)
    own = (listed, counts, blk)
    halos, done = exchange(*picked, lambda held: own_sums(*own, held=held))
    sums, weights = own_sums(*own, done=done)
    return fit(sums, weights, halos, coords_near, counts)


def solution(mesh):
    both = ("dom", "slab")
    in_specs = (
        P(None, both),
        P(None, both),
        P(None, None, both),
        P(None, both),
        P(both, None, None),
        P(both, None, None),
        P(None, both),
        P(both, None),
    )
    return jax.shard_map(local, mesh=mesh, in_specs=in_specs, out_specs=P(None, both), check_vma=False)
```

```python
import jax
import jax.numpy as jnp
import numpy as np
from jax import lax
from jax.experimental import pallas as pl
from jax.experimental.pallas import tpu as pltpu
from jax.sharding import PartitionSpec as P

RIDGE = 1.0
LANES = 128
VMEM = pl.BlockSpec(memory_space=pltpu.VMEM)
HBM = pl.BlockSpec(memory_space=pltpu.HBM)
WIDTH = 64
EDGE = 4
SUM_REACH = 2
LIMIT = 24 * 1024 * 1024


EDGES = ((0, 1), (1, 2), (0, 2), (0, 3), (1, 3), (2, 3))


def shape_table():
    near = 0.5854101966249685
    far = 0.1381966011250105
    table_rows = []
    for corner in range(4):
        barycentric = [far, far, far, far]
        barycentric[corner] = near
        values = [b * (2.0 * b - 1.0) for b in barycentric]
        values = values + [4.0 * barycentric[a] * barycentric[b] for a, b in EDGES]
        table_rows.append(values)
    return np.array(table_rows, np.float32)


SHAPE = shape_table()


def lane_gather(table, index):
    return jnp.take_along_axis(table, index, axis=1, mode="promise_in_bounds")


def rows8(ref, row, lanes):
    return jnp.broadcast_to(ref[pl.ds(row, 1), lanes], (8, LANES))


def start_all(pairs, sems):
    copies = [pltpu.make_async_copy(src, dst, sems.at[k]) for k, (src, dst) in enumerate(pairs)]
    for copy in copies:
        copy.start()
    return copies


def ninth_row(sub, table, low, high, chunks):
    total = jnp.zeros((8, LANES), jnp.float32)
    for start in range(0, chunks, 8):
        piece = lane_gather(table[start:start + 8, :], low)
        total = jnp.where(high == sub + start, piece, total)
    return total


def node_pick_kernel(
    coords_hbm, disp_hbm, send_hbm, prev_ref, next_ref, other_ref, table_ref, ninth_ref, coords_ref,
    disp_ref, send_ref, sems,
):
    pairs = ((coords_hbm, coords_ref), (disp_hbm, disp_ref), (send_hbm, send_ref))
    for copy in start_all(pairs, sems):
        copy.wait()
    sub = lax.broadcasted_iota(jnp.int32, (8, LANES), 0)
    chunks = table_ref.shape[0]
    ninth_ref[8:16, :] = jnp.zeros((8, LANES), jnp.float32)
    for chunk in range(chunks):
        lanes = pl.ds(chunk * LANES, LANES)
        table_ref[chunk, 0:3, :] = coords_ref[:, lanes]
        table_ref[chunk, 3:8, :] = disp_ref[0:5, lanes]
        ninth_ref[chunk:chunk + 1, :] = disp_ref[5:6, lanes]
    for side, out_ref in enumerate((prev_ref, next_ref, other_ref)):
        index = jnp.broadcast_to(send_ref[side], (8, LANES))
        low, high = index & 127, index >> 7
        first = jnp.zeros((8, LANES), jnp.float32)
        for chunk in range(chunks):
            first = jnp.where(high == chunk, lane_gather(table_ref[chunk], low), first)
        out_ref[0:8, :] = first
        last = ninth_row(sub, ninth_ref, low, high, chunks)
        out_ref[8:9, :] = jnp.sum(last, axis=0, keepdims=True)


def node_pick(coords, disp, send):
    out = jax.ShapeDtypeStruct((9, LANES), jnp.float32)
    chunks = coords.shape[1] // LANES
    return pl.pallas_call(
        node_pick_kernel,
        out_shape=(
            out, out, out,
            jax.ShapeDtypeStruct((chunks, 8, LANES), jnp.float32),
            jax.ShapeDtypeStruct((16, LANES), jnp.float32),
            jax.ShapeDtypeStruct(coords.shape, coords.dtype),
        ),
        in_specs=[HBM] * 3,
        out_specs=(VMEM,) * 6,
        scratch_shapes=[
            pltpu.VMEM(disp.shape, disp.dtype),
            pltpu.VMEM(send.shape, send.dtype),
            pltpu.SemaphoreType.DMA((3,)),
        ],
        compiler_params=pltpu.CompilerParams(vmem_limit_bytes=LIMIT),
        name="node_pick",
    )(coords, disp, send)


def near_edge(reach):
    return lax.rem(lax.axis_index("dom"), EDGE) < reach


def gather_work(table_ref, ninth_ref, far, near, sems):
    first_ref, last_ref, conn_ref = near[0:3]
    copies = start_all(tuple(zip(far, near[2:7])), sems)
    copies[0].wait()
    sub = lax.broadcasted_iota(jnp.int32, (8, LANES), 0)
    chunks = table_ref.shape[0]

    def group(block, carry):
        lanes = pl.ds(pl.multiple_of(block * LANES, LANES), LANES)
        for node in range(10):
            index = rows8(conn_ref, node, lanes)
            low, high = index & 127, index >> 7
            first = jnp.zeros((8, LANES), jnp.float32)
            for chunk in range(chunks):
                first = jnp.where(high == chunk, lane_gather(table_ref[chunk], low), first)
            first_ref[node, :, lanes] = first
            last = ninth_row(sub, ninth_ref, low, high, chunks)
            last_ref[node:node + 1, lanes] = jnp.sum(last, axis=0, keepdims=True)
        return carry

    lax.fori_loop(0, conn_ref.shape[1] // LANES, group, 0)
    for copy in copies[1:]:
        copy.wait()


def early_gather_kernel(*refs):
    count = (len(refs) - 15) // 2
    held, sems = refs[7:7 + count], refs[-1]
    near, outs = refs[7 + count:14 + count], refs[14 + count:14 + 2 * count]
    for source, target in zip(held, outs):
        target[...] = source[...]

    @pl.when(near_edge(1))
    def _():
        gather_work(*refs[0:2], refs[2:7], near, sems)


def late_gather_kernel(*refs):
    sems = refs[21]
    done, near = refs[7:14], refs[14:21]

    @pl.when(near_edge(1))
    def _():
        for source, target in zip(done, near):
            target[...] = source[...]

    @pl.when(jnp.logical_not(near_edge(1)))
    def _():
        gather_work(*refs[0:2], refs[2:7], near, sems)


def own_gather(table, ninth, far, held=None, done=None):
    elems = far[0].shape[1]
    outs = [jax.ShapeDtypeStruct((10, 8, elems), jnp.float32), jax.ShapeDtypeStruct((10, elems), jnp.float32)]
    outs = outs + [jax.ShapeDtypeStruct(x.shape, x.dtype) for x in far]
    extra = list(done) if held is None else list(held)
    if held is not None:
        outs = outs + [jax.ShapeDtypeStruct(x.shape, x.dtype) for x in held]
    return pl.pallas_call(
        late_gather_kernel if held is None else early_gather_kernel,
        out_shape=tuple(outs),
        in_specs=[VMEM] * 2 + [HBM] * 5 + [VMEM] * len(extra),
        out_specs=(VMEM,) * len(outs),
        scratch_shapes=[pltpu.SemaphoreType.DMA((5,))],
        compiler_params=pltpu.CompilerParams(vmem_limit_bytes=LIMIT),
        cost_estimate=pl.CostEstimate(flops=20000000, bytes_accessed=4000000, transcendentals=0),
        name="late_gather" if held is None else "early_gather",
    )(table, ninth, *far, *extra)


def block_kernel(
    first_halo, first_ref, last_ref, conn_ref, oper_ref, h0_ref, h1_ref, h2_ref, send_ref,
    blk_ref, prev_ref, next_ref, other_ref, ninth_ref, full_ref,
):
    halos = (h0_ref, h1_ref, h2_ref)
    for side, ref in enumerate(halos):
        ninth_ref[side:side + 1, :] = ref[8:9, :]
    sub = lax.broadcasted_iota(jnp.int32, (8, LANES), 0)
    groups = conn_ref.shape[1] // LANES
    ends = SHAPE[0, 1], SHAPE[0, 0] - SHAPE[0, 1]
    mids = SHAPE[0, 5], SHAPE[0, 4] - SHAPE[0, 5]

    def group(block):
        lanes = slice(block * LANES, (block + 1) * LANES)
        nodes = []
        for node in range(10):
            index = rows8(conn_ref, node, lanes)
            low, high = index & 127, index >> 7
            first = first_ref[node, :, lanes]
            for side in range(3):
                first = jnp.where(high == first_halo + side, lane_gather(halos[side][0:8, :], low), first)
            nodes.append(first)
            full_ref[block, node, 0:8, :] = first
            last = jnp.where(high == sub + first_halo, lane_gather(ninth_ref[...], low), 0.0)
            full_ref[block, node, 8:16, :] = last
        totals = [[None] * 3 for _ in range(2)]
        for node in range(10):
            for comp in range(3):
                oper = oper_ref[3 * node + comp, :, lanes].astype(jnp.float32)
                for step in range(2):
                    row = 3 + 3 * step + comp
                    value = rows8(full_ref.at[block, node], row, slice(0, LANES))
                    if row == 8:
                        value = value + rows8(last_ref, node, lanes)
                        for extra in (9, 10):
                            value = value + rows8(full_ref.at[block, node], extra, slice(0, LANES))
                    for part in range(3):
                        term = oper[8 * part:8 * part + 8] * value
                        total = totals[step][part]
                        totals[step][part] = term if total is None else total + term
        pieces = totals[0] + totals[1]
        shared = (nodes[0] + nodes[1] + nodes[2] + nodes[3]) * ends[0] + (
            nodes[4] + nodes[5] + nodes[6] + nodes[7] + nodes[8] + nodes[9]
        ) * mids[0]
        points = []
        for quad in range(4):
            a, b, c = [4 + k for k, pair in enumerate(EDGES) if quad in pair]
            points.append(shared + nodes[quad] * ends[1] + (nodes[a] + nodes[b] + nodes[c]) * mids[1])
        pieces.append(jnp.where(sub < 4, points[0], pltpu.roll(points[1], 4, 0)))
        pieces.append(jnp.where(sub < 4, points[2], pltpu.roll(points[3], 4, 0)))
        for part, piece in enumerate(pieces):
            blk_ref[8 * part:8 * part + 8, lanes] = piece

    for block in range(groups):
        group(block)
    for side, out_ref in enumerate((prev_ref, next_ref, other_ref)):
        index = jnp.broadcast_to(send_ref[side], (8, LANES))
        low, high = index & 127, index >> 7
        hits = [high == chunk for chunk in range(groups)]
        for row in range(0, 64, 8):
            total = jnp.zeros((8, LANES), jnp.float32)
            for chunk in range(groups):
                piece = blk_ref[row:row + 8, chunk * LANES:(chunk + 1) * LANES]
                total = jnp.where(hits[chunk], lane_gather(piece, low), total)
            out_ref[row:row + 8, :] = total


def make_blocks(first, last, conn, oper, halos, send, first_halo):
    elems = conn.shape[1]
    out = jax.ShapeDtypeStruct((64, LANES), jnp.float32)

    def kernel(*refs):
        block_kernel(first_halo, *refs)

    return pl.pallas_call(
        kernel,
        out_shape=(jax.ShapeDtypeStruct((64, elems), jnp.float32), out, out, out),
        in_specs=[VMEM] * 8,
        out_specs=(VMEM,) * 4,
        scratch_shapes=[
            pltpu.VMEM((8, LANES), jnp.float32),
            pltpu.VMEM((elems // LANES, 10, 16, LANES), jnp.float32),
        ],
        compiler_params=pltpu.CompilerParams(vmem_limit_bytes=LIMIT),
        name="make_blocks",
    )(first, last, conn, oper, *halos, send)


def add_points(sub, piece):
    pair = jnp.where(sub >= 6, piece[0], piece[1])
    later = jnp.where(sub >= 4, piece[1], piece[2])
    return piece[0] + pltpu.roll(pair, 2, 0) + pltpu.roll(later, 4, 0) + pltpu.roll(piece[2], 6, 0)


def moment_rows(sub, ref, lanes, out_ref, out_lanes):
    spread = []
    for dim in range(3):
        rows = [rows8(ref, 48 + 4 * quad + dim, lanes) for quad in range(4)]
        spread.append([jnp.where(sub < 6 - 2 * k, rows[k], rows[k + 1]) for k in range(3)])
    for step in range(2):
        piece = [ref[24 * step + 8 * k:24 * step + 8 * k + 8, lanes] for k in range(3)]
        base = 32 * step
        out_ref[base:base + 8, out_lanes] = add_points(sub, piece)
        for dim in range(3):
            scaled = [piece[k] * spread[dim][k] for k in range(3)]
            out_ref[base + 8 * dim + 8:base + 8 * dim + 16, out_lanes] = add_points(sub, scaled)
    pair = [ref[48:56, lanes], ref[56:64, lanes]]
    out_ref[64:72, out_lanes] = pair[0] + pair[1]
    out_ref[72:80, out_lanes] = pair[0] * pair[0] + pair[1] * pair[1]
    for shift in (1, 2):
        total = pair[0] * pltpu.roll(pair[0], 8 - shift, 0) + pair[1] * pltpu.roll(pair[1], 8 - shift, 0)
        out_ref[72 + 8 * shift:80 + 8 * shift, out_lanes] = total


def summed_over(moments, weights, weight_dim):
    rows = moments.shape[0]
    pieces, rest = [], moments
    for part in range(3):
        pieces.append(rest.astype(jnp.bfloat16))
        if part < 2:
            rest = rest - pieces[part].astype(jnp.float32)
    total = lax.dot_general(
        jnp.concatenate(pieces, axis=0), weights, (((1,), (weight_dim,)), ((), ())),
        preferred_element_type=jnp.float32,
    )
    return (total[2 * rows:] + total[rows:2 * rows]) + total[0:rows]


def sum_work(
    list_ref, count_ref, blk_ref, sum_ref, halo_ref, index_ref, hist_ref, weight_ref, moment_ref
):
    patches, slots = list_ref.shape
    counts = count_ref[...].astype(jnp.float32)
    diagonal = lax.broadcasted_iota(jnp.int32, (patches, patches), 0) == lax.broadcasted_iota(
        jnp.int32, (patches, patches), 1
    )
    spread = jnp.where(diagonal, jnp.broadcast_to(counts, (patches, patches)), 0.0)
    limits = jnp.dot(
        spread.astype(jnp.bfloat16),
        jnp.ones((patches, slots), jnp.bfloat16),
        preferred_element_type=jnp.float32,
    ).astype(jnp.int32)
    slot = lax.broadcasted_iota(jnp.int32, (patches, slots), 1)
    index_ref[...] = jnp.where(slot < limits, list_ref[...], 4095)
    low_ids = lax.broadcasted_iota(jnp.int32, (LANES, slots), 0)
    high_ids = lax.broadcasted_iota(jnp.int32, (16, slots), 0)
    width = WIDTH

    def group(block, carry):
        start = pl.multiple_of(block * width, width)
        listed = index_ref[pl.ds(start, width), :]
        low, high = listed & 127, listed >> 7
        for patch in range(width):
            low_hit = low_ids == jnp.broadcast_to(low[patch:patch + 1], (LANES, slots))
            high_hit = high_ids == jnp.broadcast_to(high[patch:patch + 1], (16, slots))
            hist = lax.dot_general(
                jnp.where(high_hit, 1.0, 0.0).astype(jnp.float8_e4m3fn),
                jnp.where(low_hit, 1.0, 0.0).astype(jnp.float8_e4m3fn),
                (((1,), (1,)), ((), ())),
                preferred_element_type=jnp.float32,
            )
            hist_ref[pl.ds(pl.multiple_of(start * 16, LANES) + 16 * patch, 16), :] = hist
        return carry

    lax.fori_loop(0, patches // width, group, 0)
    elems = blk_ref.shape[1]
    chunks = elems // LANES
    for chunk in range(chunks + 3):
        column = hist_ref[pl.ds(chunk, patches, stride=16), :]
        if chunk < chunks:
            weight_ref[:, chunk * LANES:(chunk + 1) * LANES] = column.astype(jnp.bfloat16)
        else:
            row = (chunk - chunks) * LANES
            halo_ref[row:row + LANES, :] = column.T.astype(jnp.bfloat16)
    sub = lax.broadcasted_iota(jnp.int32, (8, LANES), 0)

    def moments(block, carry):
        lanes = pl.ds(pl.multiple_of(block * LANES, LANES), LANES)
        moment_rows(sub, blk_ref, lanes, moment_ref, lanes)
        return carry

    lax.fori_loop(0, chunks, moments, 0)
    sum_ref[...] = summed_over(moment_ref[...], weight_ref[...], 1)


def early_sum_kernel(list_ref, count_ref, blk_ref, *refs):
    count = (len(refs) - 6) // 2
    sum_ref, halo_ref = refs[count:count + 2]
    scratch = refs[2 + 2 * count:]
    for source, target in zip(refs[0:count], refs[count + 2:2 * count + 2]):
        target[...] = source[...]

    @pl.when(near_edge(SUM_REACH))
    def _():
        sum_work(list_ref, count_ref, blk_ref, sum_ref, halo_ref, *scratch)


def late_sum_kernel(list_ref, count_ref, blk_ref, sum_in, halo_in, sum_ref, halo_ref, *scratch):
    @pl.when(near_edge(SUM_REACH))
    def _():
        sum_ref[...] = sum_in[...]
        halo_ref[...] = halo_in[...]

    @pl.when(jnp.logical_not(near_edge(SUM_REACH)))
    def _():
        sum_work(list_ref, count_ref, blk_ref, sum_ref, halo_ref, *scratch)


def own_sums(listed, counts, blk, held=None, done=None):
    patches, slots = listed.shape
    elems = blk.shape[1]
    outs = [
        jax.ShapeDtypeStruct((96, patches), jnp.float32),
        jax.ShapeDtypeStruct((3 * LANES, patches), jnp.bfloat16),
    ]
    extra = list(done) if held is None else list(held)
    if held is not None:
        outs = outs + [jax.ShapeDtypeStruct(x.shape, x.dtype) for x in held]
    return pl.pallas_call(
        late_sum_kernel if held is None else early_sum_kernel,
        out_shape=tuple(outs),
        in_specs=[VMEM] * (3 + len(extra)),
        out_specs=(VMEM,) * len(outs),
        scratch_shapes=[
            pltpu.VMEM((patches, slots), jnp.int32),
            pltpu.VMEM((patches * 16, LANES), jnp.float32),
            pltpu.VMEM((patches, elems), jnp.bfloat16),
            pltpu.VMEM((96, elems), jnp.float32),
        ],
        compiler_params=pltpu.CompilerParams(vmem_limit_bytes=LIMIT),
        cost_estimate=pl.CostEstimate(flops=40000000, bytes_accessed=8000000, transcendentals=0),
        name="late_sums" if held is None else "early_sums",
    )(listed, counts, blk, *extra)


def fit_kernel(sum_ref, weight_ref, h0_ref, h1_ref, h2_ref, vertex_ref, count_ref, out_ref, moment_ref, total_ref):
    sub = lax.broadcasted_iota(jnp.int32, (8, LANES), 0)
    for side, ref in enumerate((h0_ref, h1_ref, h2_ref)):
        moment_rows(sub, ref, slice(0, LANES), moment_ref, slice(side * LANES, (side + 1) * LANES))
    patches = weight_ref.shape[1]
    total_ref[...] = sum_ref[...] + summed_over(moment_ref[...], weight_ref[...], 0)

    def row(ref, start):
        return jnp.broadcast_to(ref[start:start + 1, 0:patches], (8, patches))

    def both(start):
        return row(total_ref, start) + row(total_ref, start + 4)

    points = 4.0 * row(count_ref, 0).astype(jnp.float32)
    vertex = [row(vertex_ref, dim) for dim in range(3)]
    sum_x = [both(64 + dim) for dim in range(3)]
    sum_xx = {
        (0, 0): both(72), (1, 1): both(73), (2, 2): both(74),
        (0, 1): both(80), (1, 2): both(81), (0, 2): both(88),
    }
    gram = {(0, 0): points + RIDGE}
    for a in range(3):
        gram[0, a + 1] = sum_x[a] - points * vertex[a]
        for b in range(a, 3):
            value = sum_xx[a, b] - vertex[a] * sum_x[b] - sum_x[a] * vertex[b] + points * vertex[a] * vertex[b]
            gram[a + 1, b + 1] = value + RIDGE if a == b else value
    rhs = []
    for step in range(2):
        base = total_ref[32 * step:32 * step + 8, :]
        rest = [total_ref[32 * step + 8 * dim + 8:32 * step + 8 * dim + 16, :] for dim in range(3)]
        rhs.append([base] + [rest[dim] - vertex[dim] * base for dim in range(3)])
    for pivot in (3, 2, 1):
        inverse = 1.0 / gram[pivot, pivot]
        for other in range(pivot):
            factor = gram[other, pivot] * inverse
            for column in range(other, pivot):
                gram[other, column] = gram[other, column] - factor * gram[column, pivot]
            for step in range(2):
                rhs[step][other] = rhs[step][other] - factor * rhs[step][pivot]
    inverse = 1.0 / gram[0, 0]
    for step in range(2):
        out_ref[6 * step:6 * step + 6, :] = (rhs[step][0] * inverse)[0:6]


def fit(sums, weights, halos, coords, counts):
    patches = weights.shape[1]
    return pl.pallas_call(
        fit_kernel,
        out_shape=jax.ShapeDtypeStruct((12, patches), jnp.float32),
        in_specs=[VMEM] * 7,
        out_specs=VMEM,
        scratch_shapes=[
            pltpu.VMEM((96, 3 * LANES), jnp.float32),
            pltpu.VMEM((96, patches), jnp.float32),
        ],
        compiler_params=pltpu.CompilerParams(vmem_limit_bytes=LIMIT),
        name="fit",
    )(sums, weights, *halos, coords, counts)


def exchange(to_prev, to_next, to_other, early):
    count = lax.axis_size("dom")
    up = [(i, (i + 1) % count) for i in range(count)]
    down = [(j, i) for i, j in up]
    swap = [(0, 1), (1, 0)]
    from_prev = lax.ppermute(to_next, "dom", up)
    *done, to_prev, to_other = early((to_prev, to_other))
    from_next = lax.ppermute(to_prev, "dom", down)
    from_other = lax.ppermute(to_other, "slab", swap)
    return (from_prev, from_next, from_other), done


def local(coords, disp, oper, conn, node_send, element_send, patch_elements, patch_count):
    node_send = node_send.transpose(1, 0, 2)
    element_send = element_send.transpose(1, 0, 2)
    oper = oper.transpose(1, 0, 2)
    listed = patch_elements.T
    far = [pltpu.with_memory_space_constraint(x, pltpu.HBM) for x in (
        coords, disp, node_send, conn, oper, listed, patch_count, element_send
    )]
    *picked, table, ninth, coords_near = node_pick(*far[0:3])
    own = (table, ninth, far[3:8])
    halos, done = exchange(*picked, lambda held: own_gather(*own, held=held))
    first, last, conn_near, oper, listed, counts, send = own_gather(*own, done=done)
    blk, *picked = make_blocks(first, last, conn_near, oper, halos, send, coords.shape[1] // LANES)
    own = (listed, counts, blk)
    halos, done = exchange(*picked, lambda held: own_sums(*own, held=held))
    sums, weights = own_sums(*own, done=done)
    return fit(sums, weights, halos, coords_near, counts)


def solution(mesh):
    both = ("dom", "slab")
    in_specs = (
        P(None, both),
        P(None, both),
        P(None, None, both),
        P(None, both),
        P(both, None, None),
        P(both, None, None),
        P(None, both),
        P(both, None),
    )
    return jax.shard_map(local, mesh=mesh, in_specs=in_specs, out_specs=P(None, both), check_vma=False)
```

```python
import jax
import jax.numpy as jnp
import numpy as np
from jax import lax
from jax.experimental import pallas as pl
from jax.experimental.pallas import tpu as pltpu
from jax.sharding import PartitionSpec as P

RIDGE = 1.0
LANES = 128
VMEM = pl.BlockSpec(memory_space=pltpu.VMEM)
HBM = pl.BlockSpec(memory_space=pltpu.HBM)
WIDTH = 64
EDGE = 4
HOLD = (True, False)
SUM_REACH = 1
LIMIT = 24 * 1024 * 1024


EDGES = ((0, 1), (1, 2), (0, 2), (0, 3), (1, 3), (2, 3))


def shape_table():
    near = 0.5854101966249685
    far = 0.1381966011250105
    table_rows = []
    for corner in range(4):
        barycentric = [far, far, far, far]
        barycentric[corner] = near
        values = [b * (2.0 * b - 1.0) for b in barycentric]
        values = values + [4.0 * barycentric[a] * barycentric[b] for a, b in EDGES]
        table_rows.append(values)
    return np.array(table_rows, np.float32)


SHAPE = shape_table()


def lane_gather(table, index):
    return jnp.take_along_axis(table, index, axis=1, mode="promise_in_bounds")


def rows8(ref, row, lanes):
    return jnp.broadcast_to(ref[pl.ds(row, 1), lanes], (8, LANES))


def start_all(pairs, sems):
    copies = [pltpu.make_async_copy(src, dst, sems.at[k]) for k, (src, dst) in enumerate(pairs)]
    for copy in copies:
        copy.start()
    return copies


def ninth_row(sub, table, low, high, chunks):
    total = jnp.zeros((8, LANES), jnp.float32)
    for start in range(0, chunks, 8):
        piece = lane_gather(table[start:start + 8, :], low)
        total = jnp.where(high == sub + start, piece, total)
    return total


def node_pick_kernel(
    coords_hbm, disp_hbm, send_hbm, conn_hbm,
    prev_ref, next_ref, other_ref, table_ref, ninth_ref, coords_ref, conn_ref,
    disp_ref, send_ref, sems,
):
    pairs = ((coords_hbm, coords_ref), (disp_hbm, disp_ref), (send_hbm, send_ref), (conn_hbm, conn_ref))
    copies = start_all(pairs, sems)
    for copy in copies[0:3]:
        copy.wait()
    sub = lax.broadcasted_iota(jnp.int32, (8, LANES), 0)
    chunks = table_ref.shape[0]
    ninth_ref[8:16, :] = jnp.zeros((8, LANES), jnp.float32)
    for chunk in range(chunks):
        lanes = pl.ds(chunk * LANES, LANES)
        table_ref[chunk, 0:3, :] = coords_ref[:, lanes]
        table_ref[chunk, 3:8, :] = disp_ref[0:5, lanes]
        ninth_ref[chunk:chunk + 1, :] = disp_ref[5:6, lanes]
    for side, out_ref in enumerate((prev_ref, next_ref, other_ref)):
        index = jnp.broadcast_to(send_ref[side], (8, LANES))
        low, high = index & 127, index >> 7
        first = jnp.zeros((8, LANES), jnp.float32)
        for chunk in range(chunks):
            first = jnp.where(high == chunk, lane_gather(table_ref[chunk], low), first)
        out_ref[0:8, :] = first
        last = ninth_row(sub, ninth_ref, low, high, chunks)
        out_ref[8:9, :] = jnp.sum(last, axis=0, keepdims=True)
    copies[3].wait()


def node_pick(coords, disp, send, conn):
    out = jax.ShapeDtypeStruct((9, LANES), jnp.float32)
    chunks = coords.shape[1] // LANES
    return pl.pallas_call(
        node_pick_kernel,
        out_shape=(
            out, out, out,
            jax.ShapeDtypeStruct((chunks, 8, LANES), jnp.float32),
            jax.ShapeDtypeStruct((16, LANES), jnp.float32),
            jax.ShapeDtypeStruct(coords.shape, coords.dtype),
            jax.ShapeDtypeStruct(conn.shape, conn.dtype),
        ),
        in_specs=[HBM] * 4,
        out_specs=(VMEM,) * 7,
        scratch_shapes=[
            pltpu.VMEM(disp.shape, disp.dtype),
            pltpu.VMEM(send.shape, send.dtype),
            pltpu.SemaphoreType.DMA((4,)),
        ],
        compiler_params=pltpu.CompilerParams(vmem_limit_bytes=LIMIT),
        name="node_pick",
    )(coords, disp, send, conn)


def near_edge(reach):
    return lax.rem(lax.axis_index("dom"), EDGE) < reach


def gather_work(table_ref, ninth_ref, conn_ref, far, near, sems):
    first_ref, last_ref = near[0:2]
    copies = start_all(tuple(zip(far, near[2:6])), sems)
    sub = lax.broadcasted_iota(jnp.int32, (8, LANES), 0)
    chunks = table_ref.shape[0]

    def group(block, carry):
        lanes = pl.ds(pl.multiple_of(block * LANES, LANES), LANES)
        for node in range(10):
            index = rows8(conn_ref, node, lanes)
            low, high = index & 127, index >> 7
            first = jnp.zeros((8, LANES), jnp.float32)
            for chunk in range(chunks):
                first = jnp.where(high == chunk, lane_gather(table_ref[chunk], low), first)
            first_ref[node, :, lanes] = first
            last = ninth_row(sub, ninth_ref, low, high, chunks)
            last_ref[node:node + 1, lanes] = jnp.sum(last, axis=0, keepdims=True)
        return carry

    lax.fori_loop(0, conn_ref.shape[1] // LANES, group, 0)
    for copy in copies:
        copy.wait()


def early_gather_kernel(*refs):
    count = (len(refs) - 14) // 2
    held, sems = refs[7:7 + count], refs[-1]
    near, outs = refs[7 + count:13 + count], refs[13 + count:13 + 2 * count]
    for source, target in zip(held, outs):
        target[...] = source[...]

    @pl.when(near_edge(1))
    def _():
        gather_work(*refs[0:3], refs[3:7], near, sems)


def late_gather_kernel(*refs):
    sems = refs[19]
    done, near = refs[7:13], refs[13:19]

    @pl.when(near_edge(1))
    def _():
        for source, target in zip(done, near):
            target[...] = source[...]

    @pl.when(jnp.logical_not(near_edge(1)))
    def _():
        gather_work(*refs[0:3], refs[3:7], near, sems)


def own_gather(table, ninth, conn, far, held=None, done=None):
    elems = conn.shape[1]
    outs = [jax.ShapeDtypeStruct((10, 8, elems), jnp.float32), jax.ShapeDtypeStruct((10, elems), jnp.float32)]
    outs = outs + [jax.ShapeDtypeStruct(x.shape, x.dtype) for x in far]
    extra = list(done) if held is None else list(held)
    if held is not None:
        outs = outs + [jax.ShapeDtypeStruct(x.shape, x.dtype) for x in held]
    return pl.pallas_call(
        late_gather_kernel if held is None else early_gather_kernel,
        out_shape=tuple(outs),
        in_specs=[VMEM] * 3 + [HBM] * 4 + [VMEM] * len(extra),
        out_specs=(VMEM,) * len(outs),
        scratch_shapes=[pltpu.SemaphoreType.DMA((4,))],
        compiler_params=pltpu.CompilerParams(vmem_limit_bytes=LIMIT),
        cost_estimate=pl.CostEstimate(flops=20000000, bytes_accessed=4000000, transcendentals=0),
        name="late_gather" if held is None else "early_gather",
    )(table, ninth, conn, *far, *extra)


def block_kernel(
    first_halo, first_ref, last_ref, conn_ref, oper_ref, h0_ref, h1_ref, h2_ref, send_ref,
    blk_ref, prev_ref, next_ref, other_ref, ninth_ref, full_ref,
):
    halos = (h0_ref, h1_ref, h2_ref)
    for side, ref in enumerate(halos):
        ninth_ref[side:side + 1, :] = ref[8:9, :]
    sub = lax.broadcasted_iota(jnp.int32, (8, LANES), 0)
    groups = conn_ref.shape[1] // LANES
    ends = SHAPE[0, 1], SHAPE[0, 0] - SHAPE[0, 1]
    mids = SHAPE[0, 5], SHAPE[0, 4] - SHAPE[0, 5]

    def group(block):
        lanes = slice(block * LANES, (block + 1) * LANES)
        nodes = []
        for node in range(10):
            index = rows8(conn_ref, node, lanes)
            low, high = index & 127, index >> 7
            first = first_ref[node, :, lanes]
            for side in range(3):
                first = jnp.where(high == first_halo + side, lane_gather(halos[side][0:8, :], low), first)
            nodes.append(first)
            full_ref[block, node, 0:8, :] = first
            last = jnp.where(high == sub + first_halo, lane_gather(ninth_ref[...], low), 0.0)
            full_ref[block, node, 8:16, :] = last
        totals = [[None] * 3 for _ in range(2)]
        for node in range(10):
            for comp in range(3):
                oper = oper_ref[3 * node + comp, :, lanes].astype(jnp.float32)
                for step in range(2):
                    row = 3 + 3 * step + comp
                    value = rows8(full_ref.at[block, node], row, slice(0, LANES))
                    if row == 8:
                        value = value + rows8(last_ref, node, lanes)
                        for extra in (9, 10):
                            value = value + rows8(full_ref.at[block, node], extra, slice(0, LANES))
                    for part in range(3):
                        term = oper[8 * part:8 * part + 8] * value
                        total = totals[step][part]
                        totals[step][part] = term if total is None else total + term
        pieces = totals[0] + totals[1]
        shared = (nodes[0] + nodes[1] + nodes[2] + nodes[3]) * ends[0] + (
            nodes[4] + nodes[5] + nodes[6] + nodes[7] + nodes[8] + nodes[9]
        ) * mids[0]
        points = []
        for quad in range(4):
            a, b, c = [4 + k for k, pair in enumerate(EDGES) if quad in pair]
            points.append(shared + nodes[quad] * ends[1] + (nodes[a] + nodes[b] + nodes[c]) * mids[1])
        pieces.append(jnp.where(sub < 4, points[0], pltpu.roll(points[1], 4, 0)))
        pieces.append(jnp.where(sub < 4, points[2], pltpu.roll(points[3], 4, 0)))
        for part, piece in enumerate(pieces):
            blk_ref[8 * part:8 * part + 8, lanes] = piece

    for block in range(groups):
        group(block)
    for side, out_ref in enumerate((prev_ref, next_ref, other_ref)):
        index = jnp.broadcast_to(send_ref[side], (8, LANES))
        low, high = index & 127, index >> 7
        hits = [high == chunk for chunk in range(groups)]
        for row in range(0, 64, 8):
            total = jnp.zeros((8, LANES), jnp.float32)
            for chunk in range(groups):
                piece = blk_ref[row:row + 8, chunk * LANES:(chunk + 1) * LANES]
                total = jnp.where(hits[chunk], lane_gather(piece, low), total)
            out_ref[row:row + 8, :] = total


def make_blocks(first, last, conn, oper, halos, send, first_halo):
    elems = conn.shape[1]
    out = jax.ShapeDtypeStruct((64, LANES), jnp.float32)

    def kernel(*refs):
        block_kernel(first_halo, *refs)

    return pl.pallas_call(
        kernel,
        out_shape=(jax.ShapeDtypeStruct((64, elems), jnp.float32), out, out, out),
        in_specs=[VMEM] * 8,
        out_specs=(VMEM,) * 4,
        scratch_shapes=[
            pltpu.VMEM((8, LANES), jnp.float32),
            pltpu.VMEM((elems // LANES, 10, 16, LANES), jnp.float32),
        ],
        compiler_params=pltpu.CompilerParams(vmem_limit_bytes=LIMIT),
        name="make_blocks",
    )(first, last, conn, oper, *halos, send)


def add_points(sub, piece):
    pair = jnp.where(sub >= 6, piece[0], piece[1])
    later = jnp.where(sub >= 4, piece[1], piece[2])
    return piece[0] + pltpu.roll(pair, 2, 0) + pltpu.roll(later, 4, 0) + pltpu.roll(piece[2], 6, 0)


def moment_rows(sub, ref, lanes, out_ref, out_lanes):
    spread = []
    for dim in range(3):
        rows = [rows8(ref, 48 + 4 * quad + dim, lanes) for quad in range(4)]
        spread.append([jnp.where(sub < 6 - 2 * k, rows[k], rows[k + 1]) for k in range(3)])
    for step in range(2):
        piece = [ref[24 * step + 8 * k:24 * step + 8 * k + 8, lanes] for k in range(3)]
        base = 32 * step
        out_ref[base:base + 8, out_lanes] = add_points(sub, piece)
        for dim in range(3):
            scaled = [piece[k] * spread[dim][k] for k in range(3)]
            out_ref[base + 8 * dim + 8:base + 8 * dim + 16, out_lanes] = add_points(sub, scaled)
    pair = [ref[48:56, lanes], ref[56:64, lanes]]
    out_ref[64:72, out_lanes] = pair[0] + pair[1]
    out_ref[72:80, out_lanes] = pair[0] * pair[0] + pair[1] * pair[1]
    for shift in (1, 2):
        total = pair[0] * pltpu.roll(pair[0], 8 - shift, 0) + pair[1] * pltpu.roll(pair[1], 8 - shift, 0)
        out_ref[72 + 8 * shift:80 + 8 * shift, out_lanes] = total


def summed_over(moments, weights, weight_dim):
    rows = moments.shape[0]
    pieces, rest = [], moments
    for part in range(3):
        pieces.append(rest.astype(jnp.bfloat16))
        if part < 2:
            rest = rest - pieces[part].astype(jnp.float32)
    total = lax.dot_general(
        jnp.concatenate(pieces, axis=0), weights, (((1,), (weight_dim,)), ((), ())),
        preferred_element_type=jnp.float32,
    )
    return (total[2 * rows:] + total[rows:2 * rows]) + total[0:rows]


def sum_work(
    list_ref, count_ref, blk_ref, sum_ref, halo_ref, index_ref, hist_ref, weight_ref, moment_ref
):
    patches, slots = list_ref.shape
    counts = count_ref[...].astype(jnp.float32)
    diagonal = lax.broadcasted_iota(jnp.int32, (patches, patches), 0) == lax.broadcasted_iota(
        jnp.int32, (patches, patches), 1
    )
    spread = jnp.where(diagonal, jnp.broadcast_to(counts, (patches, patches)), 0.0)
    limits = jnp.dot(
        spread.astype(jnp.bfloat16),
        jnp.ones((patches, slots), jnp.bfloat16),
        preferred_element_type=jnp.float32,
    ).astype(jnp.int32)
    slot = lax.broadcasted_iota(jnp.int32, (patches, slots), 1)
    index_ref[...] = jnp.where(slot < limits, list_ref[...], 4095)
    low_ids = lax.broadcasted_iota(jnp.int32, (LANES, slots), 0)
    high_ids = lax.broadcasted_iota(jnp.int32, (16, slots), 0)
    width = WIDTH

    def group(block, carry):
        start = pl.multiple_of(block * width, width)
        listed = index_ref[pl.ds(start, width), :]
        low, high = listed & 127, listed >> 7
        for patch in range(width):
            low_hit = low_ids == jnp.broadcast_to(low[patch:patch + 1], (LANES, slots))
            high_hit = high_ids == jnp.broadcast_to(high[patch:patch + 1], (16, slots))
            hist = lax.dot_general(
                jnp.where(high_hit, 1.0, 0.0).astype(jnp.float8_e4m3fn),
                jnp.where(low_hit, 1.0, 0.0).astype(jnp.float8_e4m3fn),
                (((1,), (1,)), ((), ())),
                preferred_element_type=jnp.float32,
            )
            hist_ref[pl.ds(pl.multiple_of(start * 16, LANES) + 16 * patch, 16), :] = hist
        return carry

    lax.fori_loop(0, patches // width, group, 0)
    elems = blk_ref.shape[1]
    chunks = elems // LANES
    for chunk in range(chunks + 3):
        column = hist_ref[pl.ds(chunk, patches, stride=16), :]
        if chunk < chunks:
            weight_ref[:, chunk * LANES:(chunk + 1) * LANES] = column.astype(jnp.bfloat16)
        else:
            row = (chunk - chunks) * LANES
            halo_ref[row:row + LANES, :] = column.T.astype(jnp.bfloat16)
    sub = lax.broadcasted_iota(jnp.int32, (8, LANES), 0)

    def moments(block, carry):
        lanes = pl.ds(pl.multiple_of(block * LANES, LANES), LANES)
        moment_rows(sub, blk_ref, lanes, moment_ref, lanes)
        return carry

    lax.fori_loop(0, chunks, moments, 0)
    sum_ref[...] = summed_over(moment_ref[...], weight_ref[...], 1)


def early_sum_kernel(list_ref, count_ref, blk_ref, *refs):
    count = (len(refs) - 6) // 2
    sum_ref, halo_ref = refs[count:count + 2]
    scratch = refs[2 + 2 * count:]
    for source, target in zip(refs[0:count], refs[count + 2:2 * count + 2]):
        target[...] = source[...]

    @pl.when(near_edge(SUM_REACH))
    def _():
        sum_work(list_ref, count_ref, blk_ref, sum_ref, halo_ref, *scratch)


def late_sum_kernel(list_ref, count_ref, blk_ref, sum_in, halo_in, sum_ref, halo_ref, *scratch):
    @pl.when(near_edge(SUM_REACH))
    def _():
        sum_ref[...] = sum_in[...]
        halo_ref[...] = halo_in[...]

    @pl.when(jnp.logical_not(near_edge(SUM_REACH)))
    def _():
        sum_work(list_ref, count_ref, blk_ref, sum_ref, halo_ref, *scratch)


def own_sums(listed, counts, blk, held=None, done=None):
    patches, slots = listed.shape
    elems = blk.shape[1]
    outs = [
        jax.ShapeDtypeStruct((96, patches), jnp.float32),
        jax.ShapeDtypeStruct((3 * LANES, patches), jnp.bfloat16),
    ]
    extra = list(done) if held is None else list(held)
    if held is not None:
        outs = outs + [jax.ShapeDtypeStruct(x.shape, x.dtype) for x in held]
    return pl.pallas_call(
        late_sum_kernel if held is None else early_sum_kernel,
        out_shape=tuple(outs),
        in_specs=[VMEM] * (3 + len(extra)),
        out_specs=(VMEM,) * len(outs),
        scratch_shapes=[
            pltpu.VMEM((patches, slots), jnp.int32),
            pltpu.VMEM((patches * 16, LANES), jnp.float32),
            pltpu.VMEM((patches, elems), jnp.bfloat16),
            pltpu.VMEM((96, elems), jnp.float32),
        ],
        compiler_params=pltpu.CompilerParams(vmem_limit_bytes=LIMIT),
        cost_estimate=pl.CostEstimate(flops=40000000, bytes_accessed=8000000, transcendentals=0),
        name="late_sums" if held is None else "early_sums",
    )(listed, counts, blk, *extra)


def fit_kernel(sum_ref, weight_ref, h0_ref, h1_ref, h2_ref, vertex_ref, count_ref, out_ref, moment_ref, total_ref):
    sub = lax.broadcasted_iota(jnp.int32, (8, LANES), 0)
    for side, ref in enumerate((h0_ref, h1_ref, h2_ref)):
        moment_rows(sub, ref, slice(0, LANES), moment_ref, slice(side * LANES, (side + 1) * LANES))
    patches = weight_ref.shape[1]
    total_ref[...] = sum_ref[...] + summed_over(moment_ref[...], weight_ref[...], 0)

    def row(ref, start):
        return jnp.broadcast_to(ref[start:start + 1, 0:patches], (8, patches))

    def both(start):
        return row(total_ref, start) + row(total_ref, start + 4)

    points = 4.0 * row(count_ref, 0).astype(jnp.float32)
    vertex = [row(vertex_ref, dim) for dim in range(3)]
    sum_x = [both(64 + dim) for dim in range(3)]
    sum_xx = {
        (0, 0): both(72), (1, 1): both(73), (2, 2): both(74),
        (0, 1): both(80), (1, 2): both(81), (0, 2): both(88),
    }
    gram = {(0, 0): points + RIDGE}
    for a in range(3):
        gram[0, a + 1] = sum_x[a] - points * vertex[a]
        for b in range(a, 3):
            value = sum_xx[a, b] - vertex[a] * sum_x[b] - sum_x[a] * vertex[b] + points * vertex[a] * vertex[b]
            gram[a + 1, b + 1] = value + RIDGE if a == b else value
    rhs = []
    for step in range(2):
        base = total_ref[32 * step:32 * step + 8, :]
        rest = [total_ref[32 * step + 8 * dim + 8:32 * step + 8 * dim + 16, :] for dim in range(3)]
        rhs.append([base] + [rest[dim] - vertex[dim] * base for dim in range(3)])
    for pivot in (3, 2, 1):
        inverse = 1.0 / gram[pivot, pivot]
        for other in range(pivot):
            factor = gram[other, pivot] * inverse
            for column in range(other, pivot):
                gram[other, column] = gram[other, column] - factor * gram[column, pivot]
            for step in range(2):
                rhs[step][other] = rhs[step][other] - factor * rhs[step][pivot]
    inverse = 1.0 / gram[0, 0]
    for step in range(2):
        out_ref[6 * step:6 * step + 6, :] = (rhs[step][0] * inverse)[0:6]


def fit(sums, weights, halos, coords, counts):
    patches = weights.shape[1]
    return pl.pallas_call(
        fit_kernel,
        out_shape=jax.ShapeDtypeStruct((12, patches), jnp.float32),
        in_specs=[VMEM] * 7,
        out_specs=VMEM,
        scratch_shapes=[
            pltpu.VMEM((96, 3 * LANES), jnp.float32),
            pltpu.VMEM((96, patches), jnp.float32),
        ],
        compiler_params=pltpu.CompilerParams(vmem_limit_bytes=LIMIT),
        name="fit",
    )(sums, weights, *halos, coords, counts)


def exchange(to_prev, to_next, to_other, early, hold):
    count = lax.axis_size("dom")
    up = [(i, (i + 1) % count) for i in range(count)]
    down = [(j, i) for i, j in up]
    swap = [(0, 1), (1, 0)]
    from_prev = lax.ppermute(to_next, "dom", up)
    if hold:
        *done, to_prev, to_other = early((to_prev, to_other))
    else:
        *done, to_prev = early((to_prev,))
    from_next = lax.ppermute(to_prev, "dom", down)
    from_other = lax.ppermute(to_other, "slab", swap)
    return (from_prev, from_next, from_other), done


def local(coords, disp, oper, conn, node_send, element_send, patch_elements, patch_count):
    node_send = node_send.transpose(1, 0, 2)
    element_send = element_send.transpose(1, 0, 2)
    oper = oper.transpose(1, 0, 2)
    listed = patch_elements.T
    far = [pltpu.with_memory_space_constraint(x, pltpu.HBM) for x in (
        coords, disp, node_send, conn, oper, listed, patch_count, element_send
    )]
    *picked, table, ninth, coords_near, conn_near = node_pick(*far[0:4])
    own = (table, ninth, conn_near, far[4:8])
    halos, done = exchange(*picked, lambda held: own_gather(*own, held=held), HOLD[0])
    first, last, oper, listed, counts, send = own_gather(*own, done=done)
    blk, *picked = make_blocks(first, last, conn_near, oper, halos, send, coords.shape[1] // LANES)
    own = (listed, counts, blk)
    halos, done = exchange(*picked, lambda held: own_sums(*own, held=held), HOLD[1])
    sums, weights = own_sums(*own, done=done)
    return fit(sums, weights, halos, coords_near, counts)


def solution(mesh):
    both = ("dom", "slab")
    in_specs = (
        P(None, both),
        P(None, both),
        P(None, None, both),
        P(None, both),
        P(both, None, None),
        P(both, None, None),
        P(None, both),
        P(both, None),
    )
    return jax.shard_map(local, mesh=mesh, in_specs=in_specs, out_specs=P(None, both), check_vma=False)
```
